256 devices in a mesh: turn: 16 (over x, z_lo), tok: 16 (over y, z_hi, core).
Axes of the slice: x: 4, y: 4, z: 8 (z_hi: 2, z_lo: 4; z = z_hi * 4 + z_lo), core: 2. Of those that a mesh axis runs over, the one named last changes fastest.
Arguments:
- activations: bfloat16 [81920, 8192], P(('turn', 'tok')), may hold values from -6 to 6
- output_grads: bfloat16 [81920, 8192], P(('turn', 'tok')), may hold values from -6 to 6
- turn_ids: int32 [81920], P(('turn', 'tok')), may hold values from 0 to 63, as said below
- turn_counts: int32 [64], P('turn'), may hold values from 640 to 3200, as said below
- input_basis: bfloat16 [8192, 256], P('tok'), may hold values from -0.0625 to 0.0625
- output_basis: bfloat16 [8192, 256], P('tok'), may hold values from -0.0625 to 0.0625
- stored_grads: bfloat16 [2048, 65536], P('turn', 'tok'), may hold values from -0.8984375 to 0.8984375
Outputs:
- scores: float32 [64, 2048], P(None, ('turn', 'tok'))
The draws below stay inside these ranges and needn't reach their ends.
Inputs may be any that keep to these rules, and one draw needn't show every extreme that they name: `turn_ids`: tokens of turn group g (the rows of the devices with turn index g) belong to turns g * 4 to g * 4 + 3 only; within one device the turn ids never fall. turn_counts[t] is the number of tokens s with turn_ids[s] == t; every turn has at least 320 * 16 // 8 tokens.
All inputs are finite; a program needn't handle non-finite values.
Results may differ from the reference program's by a relative error of at most 0.005.
Values may be sent and summed in bfloat16 or wider, within the bound.
A program may use at most 128 MiB of HBM per device.

```python
import jax
import jax.numpy as jnp
from jax import lax

D = 8192
RANK = 256
TURN_G = 4
TOK_DEV = 320
FEAT = 65536
TURNS = 64
TOKENS = 81920
ROWS = 2048
N_TURN = 16
N_TOK = 16


def turn_layout(key):
    key = jax.random.fold_in(key, 7)
    group_len = TOK_DEV * N_TOK
    base = group_len // (2 * TURN_G)
    spare = group_len - base * TURN_G

    def one_group(group):
        group_key = jax.random.fold_in(key, group)
        drawn = jnp.sort(jax.random.randint(group_key, (TURN_G - 1,), 0, spare + 1))
        cuts = jnp.where(group == 0, jnp.zeros_like(drawn), drawn)
        bounds = jnp.concatenate([jnp.zeros((1,), jnp.int32), cuts.astype(jnp.int32), jnp.full((1,), spare, jnp.int32)])
        lengths = base + (bounds[1:] - bounds[:-1])
        ends = jnp.cumsum(lengths)
        rows = jnp.arange(group_len, dtype=jnp.int32)
        stripe = rows // TOK_DEV
        within = rows % TOK_DEV
        order = within * N_TOK + stripe
        local = jnp.sum((order[:, None] >= ends[None, :]).astype(jnp.int32), axis=1)
        return (local + group * TURN_G, lengths.astype(jnp.int32))
    ids, lengths = jax.vmap(one_group)(jnp.arange(N_TURN, dtype=jnp.int32))
    return (ids.reshape(-1).astype(jnp.int32), lengths.reshape(-1).astype(jnp.int32))


def draw_turn_ids(key, part):
    return turn_layout(key)[0]


def draw_turn_counts(key, part):
    return turn_layout(key)[1]


def steps_of(rng, extent, pieces, smallest, high):
    loudness, own = 1.0, jax.random.fold_in(rng, 6)
    for axis_at, shards_of in pieces:
        heights = jnp.exp(jax.random.uniform(jax.random.fold_in(own, axis_at), (shards_of,), jnp.float32, smallest / len(pieces), high / len(pieces)))
        loudness = loudness * jnp.repeat(heights, extent[axis_at] // shards_of).reshape([-1 if axis == axis_at else 1 for axis in range(len(extent))])
    return loudness


def bell_draw(key, extent, deviation, limit, shards=(), kind=jnp.bfloat16):
    values = jax.random.normal(key, extent, jnp.float32) * deviation
    if len(shards) > 0:
        values = steps_of(key, extent, shards, -0.22, 0.18) * values
    return jnp.clip(values, min=-limit, max=limit).astype(kind)


def setup_inputs(seed: int = 0) -> dict:
    key_of = jax.random.split(jax.random.key(seed), 8)
    return {
        "activations": bell_draw(key_of[0], (TOKENS, D), 1.0, 6.0, ((0, 256),)),
        "output_grads": bell_draw(key_of[1], (TOKENS, D), 1.0, 6.0, ((0, 256),)),
        "turn_ids": draw_turn_ids(jax.random.fold_in(key_of[7], 71), 0),
        "turn_counts": draw_turn_counts(jax.random.fold_in(key_of[7], 71), 0),
        "input_basis": bell_draw(key_of[4], (D, RANK), D ** -0.5, 0.0625, ((0, 16),)),
        "output_basis": bell_draw(key_of[5], (D, RANK), D ** -0.5, 0.0625, ((0, 16),)),
        "stored_grads": bell_draw(key_of[6], (ROWS, FEAT), 0.15, 0.8984375, ((0, 16), (1, 16))),
    }


def reference(activations, output_grads, turn_ids, turn_counts, input_basis, output_basis, stored_grads):
    in_coords = jnp.dot(activations, input_basis, preferred_element_type=jnp.float32).astype(jnp.bfloat16)
    out_coords = jnp.dot(output_grads, output_basis, preferred_element_type=jnp.float32).astype(jnp.bfloat16)
    group_len = TOKENS // N_TURN

    def one_turn(turn):
        offset = (turn // TURN_G * group_len).astype(jnp.int32)
        in_part = lax.dynamic_slice_in_dim(in_coords, offset, group_len, 0)
        out_part = lax.dynamic_slice_in_dim(out_coords, offset, group_len, 0)
        id_part = lax.dynamic_slice_in_dim(turn_ids, offset, group_len, 0)
        member = (id_part == turn).astype(in_part.dtype)
        masked = out_part * member[:, None]
        return jnp.dot(masked.T, in_part, preferred_element_type=jnp.float32)

    turn_grad = lax.map(one_turn, jnp.arange(TURNS, dtype=jnp.int32))
    counts = turn_counts.astype(jnp.float32)
    turn_feat = (turn_grad / counts[:, None, None]).astype(jnp.bfloat16).reshape(TURNS, FEAT)
    return jnp.dot(turn_feat, stored_grads.T, preferred_element_type=jnp.float32)
```

```python
import functools

import jax
import jax.numpy as jnp
from jax import lax
from jax.experimental import pallas as pl
from jax.experimental.pallas import tpu as pltpu
from jax.sharding import PartitionSpec as P

TURN_G = 4
TOK = 320
TOKP = 384
D = 8192
RANK = 256
CH = 512
PC = 256
LAG = 2
EVENTS = 32
BF = jnp.bfloat16
F32 = jnp.float32
MESH = pl.DeviceIdType.MESH


def kernel(
    ids_ref,
    cnt_ref,
    act_hbm,
    og_hbm,
    ib_hbm,
    ob_hbm,
    sg_hbm,
    out_ref,
    A,
    B,
    S,
    acc,
    Gf,
    Gs,
    Hin,
    Pb,
    Rin,
    Fb,
    Ff,
    Sout,
    Q,
    s_act,
    s_own,
    s_sg,
    r_piece,
    s_sib,
    s_x,
    s_yr,
    s_yo,
    s_yz,
    s_zo,
    s_zr,
    s_h,
    r_h,
    s_rs,
    r_rs,
    s_fz,
    s_fx,
    r_f,
    s_q,
    r_q,
):
    T = lax.axis_index("turn")
    K = lax.axis_index("tok")
    x, zl = T // 4, T % 4
    y, h, c = K // 4, (K // 2) % 2, K % 2
    p = x % 2
    z = h * 4 + zl
    edge = (zl == 0) | (zl == 3)

    def tok_of(yy, hh, cc):
        return yy * 4 + hh * 2 + cc

    def zdev(zz):
        return ((x * 4 + zz % 4), tok_of(y, zz // 4, c))

    sib = (T, K + 1 - 2 * c)
    xdev = lambda d: (((x + d + 4) % 4) * 4 + zl, K)
    ydev = lambda d: (T, tok_of((y + d + 4) % 4, h, c))
    zout = zdev(jnp.where(zl == 3, (z + 1) % 8, (z + 7) % 8))
    zin = zdev(jnp.where(zl == 3, (z + 7) % 8, (z + 1) % 8))

    def rcopy(src, dst, ss, rs, dev):
        return pltpu.make_async_remote_copy(
            src_ref=src, dst_ref=dst, send_sem=ss, recv_sem=rs, device_id=dev, device_id_type=MESH
        )

    RB = TOK // 4
    loads = []
    for b, hbm in enumerate((act_hbm, og_hbm)):
        for i in range(4):
            loads.append(
                pltpu.make_async_copy(
                    hbm.at[pl.ds(i * RB, RB)], A.at[b, pl.ds(i * RB, RB)], s_act.at[b * 4 + i]
                )
            )
    own = []
    for b, hbm in enumerate((ib_hbm, ob_hbm)):
        for f in range(2):
            own.append(
                pltpu.make_async_copy(hbm.at[pl.ds(f * PC, PC)], B.at[b, K, f], s_own.at[b * 2 + f])
            )
    stored = pltpu.make_async_copy(sg_hbm, S, s_sg)
    for cp in own:
        cp.start()
    for cp in loads:
        cp.start()
    stored.start()

    barrier = pltpu.get_barrier_semaphore()

    def greet(i, _):
        pl.semaphore_signal(
            barrier, inc=1, device_id=(T, (K + i) % 16), device_id_type=MESH
        )
        pl.semaphore_signal(
            barrier, inc=1, device_id=((T + i) % 16, K), device_id_type=MESH
        )
        return 0

    lax.fori_loop(1, 16, greet, 0)

    @pl.when(edge)
    def _():
        pl.semaphore_signal(barrier, inc=1, device_id=zout, device_id_type=MESH)

    acc[...] = jnp.zeros_like(acc)
    for cp in own:
        cp.wait()

    @pl.when(edge)
    def _():
        pl.semaphore_wait(barrier, 31)

    @pl.when(jnp.logical_not(edge))
    def _():
        pl.semaphore_wait(barrier, 30)

    def piece(b, kk, f):
        return B.at[b, kk, f], r_piece.at[(b * 16 + kk) * 2 + f]

    def send(b, kk, f, sem, dev):
        ref, rs = piece(b, kk, f)
        return rcopy(ref, ref, sem, rs, dev)

    for b in range(2):
        send(b, K, p, s_yo.at[b * 2], ydev(1)).start()
        send(b, K, p, s_yo.at[b * 2 + 1], ydev(-1)).start()

    @pl.when(edge)
    def _():
        for j in range(4):
            f = p if j < 2 else 1 - p
            send(j % 2, K, f, s_zo.at[j], zout).start()

    for j in range(4):
        send(j // 2, K, j % 2, s_sib.at[j], sib).start()
    for cp in loads:
        cp.wait()

    def decode(ev):
        w = jnp.where
        i32 = jnp.int32
        is_own = ev < 4
        is_z = (ev >= 8) & (ev < 12)
        four = (ev < 8) | ((ev >= 12) & (ev < 16)) | ((ev >= 18) & (ev < 22)) | ((ev >= 24) & (ev < 28))
        base = w(ev < 4, 0, w(ev < 8, 4, w(ev < 12, 8, w(ev < 16, 12, w(ev < 18, 16, w(ev < 22, 18, w(ev < 24, 22, w(ev < 28, 24, w(ev < 30, 28, 30)))))))))
        j = ev - base
        other_h = ((ev >= 18) & (ev < 22)) | (ev >= 24)
        near = four & (ev >= 4)
        late = ev >= 28
        from_y = ((ev >= 4) & (ev < 8)) | ((ev >= 16) & (ev < 22)) | ((ev >= 28) & (ev < 30))
        b = w(is_z, j % 2, w(four, j // 2, w(late, 1 - j, j)))
        s = w(four, j % 2, j)
        yy = w(near, (y + 3 + 2 * s) % 4, (y + 2) % 4)
        hh = w(other_h, 1 - h, h)
        kk = w(is_own, K, w(is_z, tok_of(y, 1 - h, c), tok_of(yy, hh, c)))
        f = w(is_own, j % 2, w(is_z, w(j < 2, p, 1 - p), w(from_y, p, 1 - p)))
        relay = (((ev >= 4) & (ev < 8)) & (b == s)) | (((ev >= 18) & (ev < 22)) & (b != s))
        return b, kk, f, s, is_z, from_y, relay, j

    def dots(b, kk, f):
        col = pl.multiple_of(kk * CH + f * PC, PC)
        acc[b, pl.ds(0, TOK)] += jnp.dot(
            A[b, :, pl.ds(col, PC)], B[b, kk, f], preferred_element_type=F32
        )

    def step(ev, _):
        @pl.when(ev < EVENTS)
        def _():
            b, kk, f, s, is_z, from_y, relay, j = decode(ev)

            @pl.when(ev >= 4)
            def _():
                send(b, kk, f, s_sib.at[ev], sib).wait_recv()

            @pl.when(from_y)
            def _():
                d = jnp.where(s == 0, 1, -1)

                @pl.when(relay)
                def _():
                    send(b, kk, f, s_yr.at[ev], ydev(d)).start()

                send(b, kk, f, s_x.at[ev], xdev(d)).start()

            @pl.when(is_z)
            def _():
                @pl.when(edge)
                def _():
                    send(b, kk, f, s_zr.at[j], zin).start()

                @pl.when(j < 2)
                def _():
                    send(b, kk, f, s_yz.at[j * 2], ydev(1)).start()
                    send(b, kk, f, s_yz.at[j * 2 + 1], ydev(-1)).start()

            @pl.when(ev >= 4)
            def _():
                send(b, kk, f, s_sib.at[ev], sib).start()

            dots(b, kk, f)

        @pl.when(ev >= LAG)
        def _():
            b, kk, f, s, is_z, from_y, relay, j = decode(ev - LAG)
            ko = kk + 1 - 2 * c
            send(b, ko, f, s_sib.at[0], sib).wait_recv()
            dots(b, ko, f)

        return 0

    lax.fori_loop(0, EVENTS + LAG, step, 0)

    in_c = acc[0].astype(BF)
    out_t = acc[1].T
    local = ids_ref[...] - T * TURN_G
    for t in range(TURN_G):
        lhs = jnp.where(local == t, out_t, 0.0).astype(BF)
        g = jnp.dot(lhs, in_c, preferred_element_type=F32).reshape(8, 2, 16, RANK)
        for cc in range(2):
            Gf[cc, :, pl.ds(t * 16, 16), :] = g[:, cc]
            Gs[cc, :, pl.ds(t * 16, 16), :] = g[:, cc].astype(BF)
    hc = rcopy(Gs.at[1 - c], Hin, s_h, r_h, sib)
    hc.start()
    hc.wait_recv()
    me = y * 2 + h

    def rs_copy(i, m, slot):
        return rcopy(Pb.at[m], Rin.at[slot], s_rs.at[i], r_rs.at[slot], (T, m * 2 + c))

    def rs_out(i, _):
        m = (me + i) % 8
        Pb[m] = (Gf[c, m] + Hin[m].astype(F32)).astype(BF)
        rs_copy(i, m, me).start()
        return 0

    lax.fori_loop(1, 8, rs_out, 0)
    Gf[c, me] = Gf[c, me] + Hin[me].astype(F32)

    def rs_in(i, _):
        m = (me + 8 - i) % 8
        rs_copy(i, m, m).wait_recv()
        Gf[c, me] = Gf[c, me] + Rin[m].astype(F32)
        return 0

    lax.fori_loop(1, 8, rs_in, 0)
    for t in range(TURN_G):
        n = cnt_ref[t].astype(F32)
        rows = pl.ds(t * 16, 16)
        Fb[T, rows] = (Gf[c, me, rows] / n).astype(BF)

    def fz(i, zz, slot):
        return rcopy(Fb.at[slot], Fb.at[slot], s_fz.at[i], r_f.at[slot], (x * 4 + zz, K))

    def fx(i, q, xx, slot):
        return rcopy(
            Fb.at[slot], Fb.at[slot], s_fx.at[q * 4 + i], r_f.at[slot], (xx * 4 + zl, K)
        )

    def unpack(slot):
        rows = pl.ds(pl.multiple_of(slot * 64, 64), 64)
        for half in range(2):
            Ff[half, rows] = Fb[slot, :, half * 128 : (half + 1) * 128].astype(F32)

    for i in range(1, 4):
        fz(i, (zl + i) % 4, T).start()
    for i in range(1, 4):
        fx(i, 0, (x + i) % 4, T).start()
    unpack(T)

    def hand(q, _):
        zz = (zl + 4 - q) % 4
        slot = x * 4 + zz
        fz(q, zz, slot).wait_recv()
        for i in range(1, 4):
            fx(i, q, (x + i) % 4, slot).start()
        unpack(slot)
        return 0

    lax.fori_loop(1, 4, hand, 0)

    def arrive(n, _):
        q, i = n // 3, n % 3 + 1
        slot = ((x + 4 - i) % 4) * 4 + (zl + 4 - q) % 4
        fx(i, q, (x + i) % 4, slot).wait_recv()
        unpack(slot)
        return 0

    lax.fori_loop(0, 12, arrive, 0)
    stored.wait()
    sc = jnp.zeros((128, 64), F32)
    for a in range(16):
        feat = jnp.concatenate(
            [Ff[half, pl.ds(a, 64, stride=16), :] for half in range(2)], axis=1
        ).astype(BF)
        sc = sc + lax.dot_general(
            S[:, a * RANK : (a + 1) * RANK], feat, (((1,), (1,)), ((), ())), preferred_element_type=F32
        )
    Sout[:, pl.ds(0, 64)] = sc
    Sout[:, pl.ds(64, 64)] = jnp.zeros((128, 64), F32)

    def q_copy(i, k, slot):
        return rcopy(
            Sout.at[pl.ds(pl.multiple_of(k * 8, 8), 8)], Q.at[slot], s_q.at[i], r_q.at[slot], (T, k)
        )

    def q_out(i, _):
        q_copy(i, (K + i) % 16, K).start()
        return 0

    lax.fori_loop(1, 16, q_out, 0)

    def q_in(i, total):
        k = (K + 16 - i) % 16
        q_copy(i, k, k).wait_recv()
        return total + Q[k]

    total = lax.fori_loop(1, 16, q_in, Sout[pl.ds(pl.multiple_of(K * 8, 8), 8), :])
    out_ref[...] = total[:, :64]

    def done(ev, _):
        b, kk, f, s, is_z, from_y, relay, j = decode(ev)
        send(b, kk, f, s_sib.at[ev], sib).wait_send()

        @pl.when(from_y)
        def _():
            send(b, kk, f, s_x.at[ev], sib).wait_send()

        @pl.when(relay)
        def _():
            send(b, kk, f, s_yr.at[ev], sib).wait_send()

        return 0

    lax.fori_loop(0, EVENTS, done, 0)
    for i in range(4):
        send(0, K, 0, s_yo.at[i], sib).wait_send()
        send(0, K, 0, s_yz.at[i], sib).wait_send()

    @pl.when(edge)
    def _():
        for i in range(4):
            send(0, K, 0, s_zo.at[i], zout).wait_send()
            send(0, K, 0, s_zr.at[i], zin).wait_send()

    hc.wait_send()
    lax.fori_loop(1, 8, lambda i, _: (rs_copy(i, me, me).wait_send(), 0)[1], 0)
    for i in range(1, 4):
        fz(i, (zl + i) % 4, T).wait_send()
        for q in range(4):
            fx(i, q, (x + i) % 4, T).wait_send()
    lax.fori_loop(1, 16, lambda i, _: (q_copy(i, K, K).wait_send(), 0)[1], 0)


def local(
    activations, output_grads, turn_ids, turn_counts, input_basis, output_basis, stored_grads
):
    ids = jnp.pad(turn_ids, (0, TOKP - TOK), constant_values=-1).reshape(1, TOKP)
    dma = pltpu.SemaphoreType.DMA
    hbm = pl.BlockSpec(memory_space=pl.ANY)
    out = pl.pallas_call(
        kernel,
        out_shape=jax.ShapeDtypeStruct((8, 64), F32),
        in_specs=[
            pl.BlockSpec(memory_space=pltpu.VMEM),
            pl.BlockSpec(memory_space=pltpu.SMEM),
            hbm,
            hbm,
            hbm,
            hbm,
            hbm,
        ],
        out_specs=pl.BlockSpec(memory_space=pltpu.VMEM),
        scratch_shapes=[
            pltpu.VMEM((2, TOK, D), BF),
            pltpu.VMEM((2, 16, 2, PC, RANK), BF),
            pltpu.VMEM((128, 4096), BF),
            pltpu.VMEM((2, TOKP, RANK), F32),
            pltpu.VMEM((2, 8, 64, RANK), F32),
            pltpu.VMEM((2, 8, 64, RANK), BF),
            pltpu.VMEM((8, 64, RANK), BF),
            pltpu.VMEM((8, 64, RANK), BF),
            pltpu.VMEM((8, 64, RANK), BF),
            pltpu.VMEM((16, 64, RANK), BF),
            pltpu.VMEM((2, 1024, 128), F32),
            pltpu.VMEM((128, 128), F32),
            pltpu.VMEM((16, 8, 128), F32),
            dma((8,)),
            dma((4,)),
            dma,
            dma((64,)),
            dma((EVENTS,)),
            dma((EVENTS,)),
            dma((EVENTS,)),
            dma((4,)),
            dma((4,)),
            dma((4,)),
            dma((4,)),
            dma,
            dma,
            dma((8,)),
            dma((8,)),
            dma((4,)),
            dma((16,)),
            dma((16,)),
            dma((16,)),
            dma((16,)),
        ],
        compiler_params=pltpu.CompilerParams(
            collective_id=0, has_side_effects=True, vmem_limit_bytes=60 * 1024 * 1024
        ),
        cost_estimate=pl.CostEstimate(
            flops=2 * 1460000000, bytes_accessed=12 * 1024 * 1024, transcendentals=0
        ),
    )(
        ids,
        turn_counts,
        activations,
        output_grads,
        input_basis,
        output_basis,
        stored_grads,
    )
    return out.T


def solution(mesh):
    placed = (
        P(("turn", "tok"), None),
        P(("turn", "tok"), None),
        P(("turn", "tok")),
        P("turn"),
        P("tok", None),
        P("tok", None),
        P("turn", "tok"),
    )
    return jax.shard_map(
        local, mesh=mesh, in_specs=placed, out_specs=P(None, ("turn", "tok")), check_vma=False
    )
```

```python
import functools

import jax
import jax.numpy as jnp
from jax import lax
from jax.experimental import pallas as pl
from jax.experimental.pallas import tpu as pltpu
from jax.sharding import PartitionSpec as P

TURN_G = 4
TOK = 320
TOKP = 384
D = 8192
RANK = 256
CH = 512
PC = 256
NS = 2
ORDER = (
    8, 24, 9, 25, 4, 40, 56, 10, 26, 41, 57, 5, 11, 27, 12, 42,
    58, 16, 36, 43, 59, 17, 28, 48, 14, 13, 29, 49, 37, 18, 60, 6,
    19, 30, 50, 20, 44, 7, 15, 31, 51, 61, 38, 62, 52, 21, 45, 39,
    22, 46, 53, 63, 54, 23, 47, 55,
)
HALVES = ((1, 0, 0), (3, 0, 0), (1, 0, 1), (3, 0, 1), (2, 0, 0), (0, 1, 0), (2, 0, 1), (3, 1, 0), (1, 1, 0), (0, 1, 1), (2, 1, 0), (3, 1, 1), (1, 1, 1), (2, 1, 1))
SEND_MAX = 4 * NS + 4 * NS + len(ORDER) * 2
LAG = 2 * NS
BF = jnp.bfloat16
F32 = jnp.float32
MESH = pl.DeviceIdType.MESH


def kernel(
    ids_ref,
    cnt_ref,
    act_hbm,
    og_hbm,
    ib_hbm,
    ob_hbm,
    sg_hbm,
    out_ref,
    A,
    B,
    S,
    acc,
    ids,
    Gf,
    Gs,
    Hin,
    Pb,
    Rin,
    Fb,
    Ff,
    Sout,
    Q,
    s_act,
    s_own,
    s_sg,
    r_piece,
    r_sib,
    s_sib,
    s_fwd,
    s_out,
    s_h,
    r_h,
    s_rs,
    r_rs,
    s_fz,
    s_fx,
    r_f,
    s_q,
    r_q,
):
    T = lax.axis_index("turn")
    K = lax.axis_index("tok")
    x, zl = T // 4, T % 4
    y, h, c = K // 4, (K // 2) % 2, K % 2
    z = h * 4 + zl
    edge = (zl == 0) | (zl == 3)
    inner = ((zl + 1) // 2) % 2
    p = (x + inner) % 2
    def tok_of(yy, hh, cc):
        return yy * 4 + hh * 2 + cc

    def zdev(zz):
        return ((x * 4 + zz % 4), tok_of(y, zz // 4, c))

    sib = (T, K + 1 - 2 * c)
    xdev = lambda d: (((x + d + 4) % 4) * 4 + zl, K)
    ydev = lambda d: (T, tok_of((y + d + 4) % 4, h, c))
    pair = (x * 4 + zl + 1 - 2 * (zl % 2), K)
    up = jnp.where(zl >= 2, 1, 7)
    over1 = zdev((z + up) % 8)
    over2 = zdev((z + up * 2) % 8)

    def rcopy(src, dst, ss, rs, dev):
        return pltpu.make_async_remote_copy(
            src_ref=src, dst_ref=dst, send_sem=ss, recv_sem=rs, device_id=dev, device_id_type=MESH
        )

    RB = TOK // 4
    R = PC // NS
    loads = []
    for b, hbm in enumerate((act_hbm, og_hbm)):
        for i in range(4):
            loads.append(
                pltpu.make_async_copy(
                    hbm.at[pl.ds(i * RB, RB)], A.at[b, pl.ds(i * RB, RB)], s_act.at[b * 4 + i]
                )
            )
    own = []
    for b, hbm in enumerate((ib_hbm, ob_hbm)):
        for f in range(2):
            own.append(
                pltpu.make_async_copy(hbm.at[pl.ds(f * PC, PC)], B.at[b, K, f], s_own.at[b * 2 + f])
            )
    stored = pltpu.make_async_copy(sg_hbm, S, s_sg)
    for cp in own:
        cp.start()
    for cp in loads:
        cp.start()
    stored.start()

    barrier = pltpu.get_barrier_semaphore()

    def greet(i, _):
        pl.semaphore_signal(
            barrier, inc=1, device_id=(T, (K + i) % 16), device_id_type=MESH
        )
        pl.semaphore_signal(
            barrier, inc=1, device_id=((T + i) % 16, K), device_id_type=MESH
        )
        return 0

    lax.fori_loop(1, 16, greet, 0)

    pl.semaphore_signal(barrier, inc=1, device_id=over2, device_id_type=MESH)

    @pl.when(edge)
    def _():
        pl.semaphore_signal(barrier, inc=1, device_id=over1, device_id_type=MESH)

    acc[...] = jnp.zeros_like(acc)
    ids[...] = jnp.full_like(ids, -1)
    ids[:, pl.ds(0, TOK)] = ids_ref[...]
    for cp in own:
        cp.wait()

    @pl.when(edge)
    def _():
        pl.semaphore_wait(barrier, 32)

    @pl.when(jnp.logical_not(edge))
    def _():
        pl.semaphore_wait(barrier, 31)

    def part(b, kk, f, i):
        return B.at[b, kk, f, pl.ds(i * R, R)], r_piece.at[((b * 16 + kk) * 2 + f) * NS + i]

    sent = []

    def send(b, kk, f, i, dev):
        ref, rs = part(b, kk, f, i)
        cp = rcopy(ref, ref, s_fwd.at[len(sent)], rs, dev)
        cp.start()
        sent.append(cp)

    for b in range(2):
        for i in range(NS):
            send(b, K, p, i, ydev(1))
            send(b, K, p, i, ydev(-1))

    def boundary():
        out = []
        for b in range(2):
            for i in range(NS):
                for far, (dev, f) in enumerate(((over1, p), (over2, 1 - p))):
                    ref, rs = part(b, K, f, i)
                    out.append(rcopy(ref, ref, s_out.at[(b * NS + i) * 2 + far], rs, dev))
        return out

    @pl.when(edge)
    def _():
        for cp in boundary():
            cp.start()

    shared = []

    def share(b, kk, f):
        ref = B.at[b, kk] if f is None else B.at[b, kk, f]
        rs = r_sib.at[(b * 16 + kk) * 2 + (0 if f is None else f)]
        cp = rcopy(ref, ref, s_sib.at[len(shared)], rs, sib)
        cp.start()
        shared.append(cp)

    def share_wait(b, kk, f):
        ref = B.at[b, kk] if f is None else B.at[b, kk, f]
        rs = r_sib.at[(b * 16 + kk) * 2 + (0 if f is None else f)]
        rcopy(ref, ref, s_sib.at[0], rs, sib).wait_recv()

    for b in range(2):
        share(b, K, None)
    KO = K + 1 - 2 * c

    def place(dy, dh, half):
        hh = h if dh == 0 else 1 - h
        return tok_of((y + dy) % 4, hh, c), (p if half == 0 else 1 - p)

    def dots(b, blocks):
        lhs, rhs = [], []
        for kk, f in blocks:
            col = pl.multiple_of(kk * CH + f * PC, PC)
            lhs.append(A[b, :, pl.ds(col, PC)])
            rhs.append(B[b, kk, f])
        acc[b, pl.ds(0, TOK)] += jnp.dot(
            jnp.concatenate(lhs, axis=1), jnp.concatenate(rhs, axis=0), preferred_element_type=F32
        )

    def dots_of(b, group):
        if group == 0:
            if b == 0:
                for cp in loads[:4]:
                    cp.wait()
            else:
                for cp in loads[4:]:
                    cp.wait()
            share_wait(b, KO, None)
            dots(b, [(K, 0), (K, 1), (KO, 0), (KO, 1)])
            return
        blocks = []
        for q in HALVES[2 * group - 2 : 2 * group]:
            kk, f = place(*q)
            ko = kk + 1 - 2 * c
            share_wait(b, ko, f)
            blocks += [(kk, f), (ko, f)]
        dots(b, blocks)

    seen = [{}, {}]
    for n, code in enumerate(ORDER):
        i, half, dh, dy, b = code % NS, code // NS % 2, code // NS // 2 % 2, code // NS // 4 % 4, code // NS // 16
        seen[b][(dy, dh, half)] = n
    due = []
    for b in range(2):
        due.append((NS + NS * b, b, 0))
        for group in range(1, 8):
            last = max(seen[b][q] for q in HALVES[2 * group - 2 : 2 * group])
            due.append((last + LAG, b, group))
    due.sort(key=lambda e: (e[0], e[2]))

    parts = {}
    for n, code in enumerate(ORDER):
        i, half, dh, dy, b = code % NS, code // NS % 2, code // NS // 2 % 2, code // NS // 4 % 4, code // NS // 16
        kk, f = place(dy, dh, half)
        ref, rs = part(b, kk, f, i)
        rcopy(ref, ref, s_fwd.at[0], rs, sib).wait_recv()
        if dy == 0:
            if half == 0:
                send(b, kk, f, i, ydev(1))
                send(b, kk, f, i, ydev(-1))
                send(b, kk, f, i, pair)
        elif half == 0:
            side = {3: 0, 1: 1, 2: b if dh == 0 else 1 - b}[dy]
            d = 1 if side == 0 else -1
            if dy != 2 and (b == side) == (dh == 0):
                send(b, kk, f, i, ydev(d))
            send(b, kk, f, i, xdev(d))
        got = parts.setdefault((b, dy, dh, half), set())
        got.add(i)
        if len(got) == NS:
            share(b, kk, f)
        while due and due[0][0] <= n:
            _, bb, group = due.pop(0)
            dots_of(bb, group)
    for _, bb, group in due:
        dots_of(bb, group)

    in_c = acc[0].astype(BF)
    out_t = acc[1].T
    local = ids[...] - T * TURN_G
    for t in range(TURN_G):
        lhs = jnp.where(local == t, out_t, 0.0).astype(BF)
        g = jnp.dot(lhs, in_c, preferred_element_type=F32).reshape(8, 2, 16, RANK)
        for cc in range(2):
            Gf[cc, :, pl.ds(t * 16, 16), :] = g[:, cc]
            Gs[cc, :, pl.ds(t * 16, 16), :] = g[:, cc].astype(BF)
    hc = rcopy(Gs.at[1 - c], Hin, s_h, r_h, sib)
    hc.start()
    hc.wait_recv()
    me = y * 2 + h

    def rs_copy(i, m, slot):
        return rcopy(Pb.at[m], Rin.at[slot], s_rs.at[i], r_rs.at[slot], (T, m * 2 + c))

    def rs_out(i, _):
        m = (me + i) % 8
        Pb[m] = (Gf[c, m] + Hin[m].astype(F32)).astype(BF)
        rs_copy(i, m, me).start()
        return 0

    lax.fori_loop(1, 8, rs_out, 0)
    for cp in sent + shared:
        cp.wait_send()

    @pl.when(edge)
    def _():
        for cp in boundary():
            cp.wait_send()

    Gf[c, me] = Gf[c, me] + Hin[me].astype(F32)

    def rs_in(i, _):
        m = (me + 8 - i) % 8
        rs_copy(i, m, m).wait_recv()
        Gf[c, me] = Gf[c, me] + Rin[m].astype(F32)
        return 0

    lax.fori_loop(1, 8, rs_in, 0)
    for t in range(TURN_G):
        n = cnt_ref[t].astype(F32)
        rows = pl.ds(t * 16, 16)
        Fb[T, rows] = (Gf[c, me, rows] / n).astype(BF)

    def fz(i, zz, slot):
        return rcopy(Fb.at[slot], Fb.at[slot], s_fz.at[i], r_f.at[slot], (x * 4 + zz, K))

    def fx(i, q, xx, slot):
        return rcopy(
            Fb.at[slot], Fb.at[slot], s_fx.at[q * 4 + i], r_f.at[slot], (xx * 4 + zl, K)
        )

    def unpack(slot):
        rows = pl.ds(pl.multiple_of(slot * 64, 64), 64)
        for half in range(2):
            Ff[half, rows] = Fb[slot, :, half * 128 : (half + 1) * 128].astype(F32)

    for i in range(1, 4):
        fz(i, (zl + i) % 4, T).start()
    for i in range(1, 4):
        fx(i, 0, (x + i) % 4, T).start()
    unpack(T)

    def hand(q, _):
        zz = (zl + 4 - q) % 4
        slot = x * 4 + zz
        fz(q, zz, slot).wait_recv()
        for i in range(1, 4):
            fx(i, q, (x + i) % 4, slot).start()
        unpack(slot)
        return 0

    lax.fori_loop(1, 4, hand, 0)

    def arrive(n, _):
        q, i = n // 3, n % 3 + 1
        slot = ((x + 4 - i) % 4) * 4 + (zl + 4 - q) % 4
        fx(i, q, (x + i) % 4, slot).wait_recv()
        unpack(slot)
        return 0

    lax.fori_loop(0, 12, arrive, 0)
    stored.wait()
    sc = jnp.zeros((128, 64), F32)
    for a in range(16):
        feat = jnp.concatenate(
            [Ff[half, pl.ds(a, 64, stride=16), :] for half in range(2)], axis=1
        ).astype(BF)
        sc = sc + lax.dot_general(
            S[:, a * RANK : (a + 1) * RANK], feat, (((1,), (1,)), ((), ())), preferred_element_type=F32
        )
    Sout[:, pl.ds(0, 64)] = sc
    Sout[:, pl.ds(64, 64)] = jnp.zeros((128, 64), F32)

    def q_copy(i, k, slot):
        return rcopy(
            Sout.at[pl.ds(pl.multiple_of(k * 8, 8), 8)], Q.at[slot], s_q.at[i], r_q.at[slot], (T, k)
        )

    def q_out(i, _):
        q_copy(i, (K + i) % 16, K).start()
        return 0

    lax.fori_loop(1, 16, q_out, 0)

    def q_in(i, total):
        k = (K + 16 - i) % 16
        q_copy(i, k, k).wait_recv()
        return total + Q[k]

    total = lax.fori_loop(1, 16, q_in, Sout[pl.ds(pl.multiple_of(K * 8, 8), 8), :])
    out_ref[...] = total[:, :64]

    hc.wait_send()
    lax.fori_loop(1, 8, lambda i, _: (rs_copy(i, me, me).wait_send(), 0)[1], 0)
    for i in range(1, 4):
        fz(i, (zl + i) % 4, T).wait_send()
        for q in range(4):
            fx(i, q, (x + i) % 4, T).wait_send()
    lax.fori_loop(1, 16, lambda i, _: (q_copy(i, K, K).wait_send(), 0)[1], 0)


def local(
    activations, output_grads, turn_ids, turn_counts, input_basis, output_basis, stored_grads
):
    ids = turn_ids.reshape(1, TOK)
    dma = pltpu.SemaphoreType.DMA
    hbm = pl.BlockSpec(memory_space=pl.ANY)
    out = pl.pallas_call(
        kernel,
        out_shape=jax.ShapeDtypeStruct((8, 64), F32),
        in_specs=[
            pl.BlockSpec(memory_space=pltpu.VMEM),
            pl.BlockSpec(memory_space=pltpu.SMEM),
            hbm,
            hbm,
            hbm,
            hbm,
            hbm,
        ],
        out_specs=pl.BlockSpec(memory_space=pltpu.VMEM),
        scratch_shapes=[
            pltpu.VMEM((2, TOK, D), BF),
            pltpu.VMEM((2, 16, 2, PC, RANK), BF),
            pltpu.VMEM((128, 4096), BF),
            pltpu.VMEM((2, TOKP, RANK), F32),
            pltpu.VMEM((1, TOKP), jnp.int32),
            pltpu.VMEM((2, 8, 64, RANK), F32),
            pltpu.VMEM((2, 8, 64, RANK), BF),
            pltpu.VMEM((8, 64, RANK), BF),
            pltpu.VMEM((8, 64, RANK), BF),
            pltpu.VMEM((8, 64, RANK), BF),
            pltpu.VMEM((16, 64, RANK), BF),
            pltpu.VMEM((2, 1024, 128), F32),
            pltpu.VMEM((128, 128), F32),
            pltpu.VMEM((16, 8, 128), F32),
            dma((8,)),
            dma((4,)),
            dma,
            dma((64 * NS,)),
            dma((64,)),
            dma((32,)),
            dma((SEND_MAX,)),
            dma((4 * NS,)),
            dma,
            dma,
            dma((8,)),
            dma((8,)),
            dma((4,)),
            dma((16,)),
            dma((16,)),
            dma((16,)),
            dma((16,)),
        ],
        compiler_params=pltpu.CompilerParams(
            collective_id=0, has_side_effects=True, vmem_limit_bytes=60 * 1024 * 1024
        ),
        cost_estimate=pl.CostEstimate(
            flops=2 * 1460000000, bytes_accessed=12 * 1024 * 1024, transcendentals=0
        ),
    )(
        ids,
        turn_counts,
        activations,
        output_grads,
        input_basis,
        output_basis,
        stored_grads,
    )
    return out.T


def solution(mesh):
    placed = (
        P(("turn", "tok"), None),
        P(("turn", "tok"), None),
        P(("turn", "tok")),
        P("turn"),
        P("tok", None),
        P("tok", None),
        P("turn", "tok"),
    )
    return jax.shard_map(
        local, mesh=mesh, in_specs=placed, out_specs=P(None, ("turn", "tok")), check_vma=False
    )
```

```python
import functools

import jax
import jax.numpy as jnp
from jax import lax
from jax.experimental import pallas as pl
from jax.experimental.pallas import tpu as pltpu
from jax.sharding import PartitionSpec as P

TURN_G = 4
TOK = 320
TOKP = 384
D = 8192
RANK = 256
CH = 512
PC = 256
NS = 2
ORDER = (
    8, 24, 9, 25, 4, 40, 56, 5, 10, 41, 57, 16, 12, 17, 26, 48,
    36, 28, 13, 37, 14, 49, 29, 60, 20, 61, 44, 50, 21, 27, 43, 52,
    45, 53, 58, 46, 63, 15, 23, 6, 62, 19, 39, 42, 22, 54, 7, 38,
    11, 30, 51, 59, 31, 18, 47, 55,
)
HALVES = ((1, 0, 0), (3, 0, 0), (0, 1, 0), (2, 0, 0), (3, 1, 0), (1, 1, 0), (2, 1, 0), (0, 1, 1), (1, 0, 1), (3, 0, 1), (3, 1, 1), (2, 0, 1), (1, 1, 1), (2, 1, 1))
SEND_MAX = 4 * NS + 4 * NS + len(ORDER) * 2
LAG = 3
BF = jnp.bfloat16
F32 = jnp.float32
MESH = pl.DeviceIdType.MESH


def kernel(
    ids_ref,
    cnt_ref,
    act_hbm,
    og_hbm,
    ib_hbm,
    ob_hbm,
    sg_hbm,
    out_ref,
    A,
    B,
    S,
    acc,
    ids,
    OT,
    Gf,
    Gs,
    Hin,
    Pb,
    Rin,
    Fb,
    Ff,
    Sout,
    Qh,
    Sc,
    Q,
    s_act,
    s_own,
    s_sg,
    r_piece,
    r_sib,
    s_sib,
    s_fwd,
    s_out,
    s_h,
    r_h,
    s_rs,
    r_rs,
    s_fz,
    s_fx,
    r_f,
    s_qh,
    r_qh,
    s_q,
    r_q,
):
    T = lax.axis_index("turn")
    K = lax.axis_index("tok")
    x, zl = T // 4, T % 4
    y, h, c = K // 4, (K // 2) % 2, K % 2
    z = h * 4 + zl
    edge = (zl == 0) | (zl == 3)
    inner = ((zl + 1) // 2) % 2
    p = (x + inner) % 2
    def tok_of(yy, hh, cc):
        return yy * 4 + hh * 2 + cc

    def zdev(zz):
        return ((x * 4 + zz % 4), tok_of(y, zz // 4, c))

    sib = (T, K + 1 - 2 * c)
    xdev = lambda d: (((x + d + 4) % 4) * 4 + zl, K)
    ydev = lambda d: (T, tok_of((y + d + 4) % 4, h, c))
    pair = (x * 4 + zl + 1 - 2 * (zl % 2), K)
    up = jnp.where(zl >= 2, 1, 7)
    over1 = zdev((z + up) % 8)
    over2 = zdev((z + up * 2) % 8)

    def rcopy(src, dst, ss, rs, dev):
        return pltpu.make_async_remote_copy(
            src_ref=src, dst_ref=dst, send_sem=ss, recv_sem=rs, device_id=dev, device_id_type=MESH
        )

    RB = TOK // 4
    R = PC // NS
    loads = []
    for b, hbm in enumerate((act_hbm, og_hbm)):
        for i in range(4):
            loads.append(
                pltpu.make_async_copy(
                    hbm.at[pl.ds(i * RB, RB)], A.at[b, pl.ds(i * RB, RB)], s_act.at[b * 4 + i]
                )
            )
    own = []
    for b, hbm in enumerate((ib_hbm, ob_hbm)):
        for f in range(2):
            own.append(
                pltpu.make_async_copy(hbm.at[pl.ds(f * PC, PC)], B.at[b, K, f], s_own.at[b * 2 + f])
            )
    stored = pltpu.make_async_copy(sg_hbm, S, s_sg)
    for cp in own:
        cp.start()
    for cp in loads:
        cp.start()
    stored.start()

    barrier = pltpu.get_barrier_semaphore()

    def greet(i, _):
        pl.semaphore_signal(
            barrier, inc=1, device_id=(T, (K + i) % 16), device_id_type=MESH
        )
        pl.semaphore_signal(
            barrier, inc=1, device_id=((T + i) % 16, K), device_id_type=MESH
        )
        return 0

    lax.fori_loop(1, 16, greet, 0)

    pl.semaphore_signal(barrier, inc=1, device_id=over2, device_id_type=MESH)

    @pl.when(edge)
    def _():
        pl.semaphore_signal(barrier, inc=1, device_id=over1, device_id_type=MESH)

    acc[...] = jnp.zeros_like(acc)
    ids[...] = jnp.full_like(ids, -1)
    ids[0, pl.ds(0, TOK)] = ids_ref[...]
    Sout[...] = jnp.zeros_like(Sout)
    for cp in own:
        cp.wait()

    @pl.when(edge)
    def _():
        pl.semaphore_wait(barrier, 32)

    @pl.when(jnp.logical_not(edge))
    def _():
        pl.semaphore_wait(barrier, 31)

    def part(b, kk, f, i):
        return B.at[b, kk, f, pl.ds(i * R, R)], r_piece.at[((b * 16 + kk) * 2 + f) * NS + i]

    sent = []

    def send(b, kk, f, i, dev):
        ref, rs = part(b, kk, f, i)
        cp = rcopy(ref, ref, s_fwd.at[len(sent)], rs, dev)
        cp.start()
        sent.append(cp)

    for b in range(2):
        for i in range(NS):
            send(b, K, p, i, ydev(1))
            send(b, K, p, i, ydev(-1))

    def boundary():
        out = []
        for b in range(2):
            for i in range(NS):
                for far, (dev, f) in enumerate(((over1, p), (over2, 1 - p))):
                    ref, rs = part(b, K, f, i)
                    out.append(rcopy(ref, ref, s_out.at[(b * NS + i) * 2 + far], rs, dev))
        return out

    @pl.when(edge)
    def _():
        for cp in boundary():
            cp.start()

    shared = []

    def share(b, kk, f):
        ref = B.at[b, kk] if f is None else B.at[b, kk, f]
        rs = r_sib.at[(b * 16 + kk) * 2 + (0 if f is None else f)]
        cp = rcopy(ref, ref, s_sib.at[len(shared)], rs, sib)
        cp.start()
        shared.append(cp)

    def share_wait(b, kk, f):
        ref = B.at[b, kk] if f is None else B.at[b, kk, f]
        rs = r_sib.at[(b * 16 + kk) * 2 + (0 if f is None else f)]
        rcopy(ref, ref, s_sib.at[0], rs, sib).wait_recv()

    for b in range(2):
        share(b, K, None)
    KO = K + 1 - 2 * c

    def place(dy, dh, half):
        hh = h if dh == 0 else 1 - h
        return tok_of((y + dy) % 4, hh, c), (p if half == 0 else 1 - p)

    def dots(b, blocks):
        lhs, rhs = [], []
        for kk, f in blocks:
            col = pl.multiple_of(kk * CH + f * PC, PC)
            lhs.append(A[b, :, pl.ds(col, PC)])
            rhs.append(B[b, kk, f])
        acc[b, pl.ds(0, TOK)] += jnp.dot(
            jnp.concatenate(lhs, axis=1), jnp.concatenate(rhs, axis=0), preferred_element_type=F32
        )

    def dots_of(b, group):
        if group == 0:
            if b == 0:
                for cp in loads[:4]:
                    cp.wait()
            else:
                for cp in loads[4:]:
                    cp.wait()
            share_wait(b, KO, None)
            dots(b, [(K, 0), (K, 1), (KO, 0), (KO, 1)])
            return
        blocks = [place(*q) for q in HALVES[2 * group - 2 : 2 * group]]
        others = [(kk + 1 - 2 * c, f) for kk, f in blocks]
        if group == 7:
            dots(b, blocks)
            blocks = []
        for ko, f in others:
            share_wait(b, ko, f)
        dots(b, blocks + others)

    seen = [{}, {}]
    for n, code in enumerate(ORDER):
        i, half, dh, dy, b = code % NS, code // NS % 2, code // NS // 2 % 2, code // NS // 4 % 4, code // NS // 16
        seen[b][(dy, dh, half)] = n
    due = []
    for b in range(2):
        due.append((NS + NS * b, b, 0))
        for group in range(1, 8):
            last = max(seen[b][q] for q in HALVES[2 * group - 2 : 2 * group])
            due.append((last + LAG, b, group))
    due.sort(key=lambda e: (e[0], e[2]))

    parts = {}
    for n, code in enumerate(ORDER):
        i, half, dh, dy, b = code % NS, code // NS % 2, code // NS // 2 % 2, code // NS // 4 % 4, code // NS // 16
        kk, f = place(dy, dh, half)
        ref, rs = part(b, kk, f, i)
        rcopy(ref, ref, s_fwd.at[0], rs, sib).wait_recv()
        if dy == 0:
            if half == 0:
                send(b, kk, f, i, ydev(1))
                send(b, kk, f, i, ydev(-1))
                send(b, kk, f, i, pair)
        elif half == 0:
            side = {3: 0, 1: 1, 2: b if dh == 0 else 1 - b}[dy]
            d = 1 if side == 0 else -1
            if dy != 2 and (b == side) == (dh == 0):
                send(b, kk, f, i, ydev(d))
            send(b, kk, f, i, xdev(d))
        got = parts.setdefault((b, dy, dh, half), set())
        got.add(i)
        if len(got) == NS:
            share(b, kk, f)
        while due and due[0][0] <= n:
            _, bb, group = due.pop(0)
            dots_of(bb, group)
    for _, bb, group in due:
        dots_of(bb, group)

    in_c = acc[0].astype(BF)
    out_t = acc[1].T.reshape(8, 2, 16, TOKP)
    for cc in range(2):
        OT[cc] = out_t[:, cc].reshape(128, TOKP)
    local = ids[...] - T * TURN_G

    def gradient(cc, t):
        lhs = jnp.where(local == t, OT[cc], 0.0).astype(BF)
        return jnp.dot(lhs, in_c, preferred_element_type=F32).reshape(8, 16, RANK)

    for t in range(TURN_G):
        Gs[:, pl.ds(t * 16, 16), :] = gradient(1 - c, t).astype(BF)
    hc = rcopy(Gs, Hin, s_h, r_h, sib)
    hc.start()
    for t in range(TURN_G):
        Gf[:, pl.ds(t * 16, 16), :] = gradient(c, t)
    hc.wait_recv()
    me = y * 2 + h

    def peer(i, sign):
        far = i < 4
        yy = (y + 4 + sign * jnp.where(far, i, i - 3)) % 4
        return yy * 2 + jnp.where(far, 1 - h, h)

    def rs_copy(i, m, slot):
        return rcopy(Pb.at[m], Rin.at[slot], s_rs.at[i], r_rs.at[slot], (T, m * 2 + c))

    def rs_out(i, _):
        m = peer(i, 1)
        Pb[m] = (Gf[m] + Hin[m].astype(F32)).astype(BF)
        rs_copy(i, m, me).start()
        return 0

    lax.fori_loop(0, 7, rs_out, 0)
    Gf[me] = Gf[me] + Hin[me].astype(F32)
    for cp in sent + shared:
        cp.wait_send()

    @pl.when(edge)
    def _():
        for cp in boundary():
            cp.wait_send()

    hc.wait_send()

    def rs_in(i, _):
        m = peer(6 - i, -1)
        rs_copy(0, m, m).wait_recv()
        Gf[me] = Gf[me] + Rin[m].astype(F32)
        return 0

    lax.fori_loop(0, 7, rs_in, 0)
    for t in range(TURN_G):
        n = cnt_ref[t].astype(F32)
        rows = pl.ds(t * 16, 16)
        Fb[T, rows] = (Gf[me, rows] / n).astype(BF)

    def fz(i, zz, slot):
        return rcopy(Fb.at[slot], Fb.at[slot], s_fz.at[i], r_f.at[slot], (x * 4 + zz, K))

    def fx(i, q, xx, slot):
        return rcopy(
            Fb.at[slot], Fb.at[slot], s_fx.at[q * 4 + i], r_f.at[slot], (xx * 4 + zl, K)
        )

    def unpack(slot):
        rows = pl.ds(pl.multiple_of(slot * 64, 64), 64)
        for half in range(2):
            Ff[half, rows] = Fb[slot, :, half * 128 : (half + 1) * 128].astype(F32)

    for i in range(1, 4):
        fz(i, (zl + i) % 4, T).start()
    for i in range(1, 4):
        fx(i, 0, (x + i) % 4, T).start()
    unpack(T)
    lax.fori_loop(0, 7, lambda i, _: (rs_copy(i, me, me).wait_send(), 0)[1], 0)

    def hand(q, _):
        zz = (zl + 4 - q) % 4
        slot = x * 4 + zz
        fz(q, zz, slot).wait_recv()
        for i in range(1, 4):
            fx(i, q, (x + i) % 4, slot).start()
        unpack(slot)
        return 0

    lax.fori_loop(1, 4, hand, 0)

    def arrive(n, _):
        q, i = n // 3, n % 3 + 1
        slot = ((x + 4 - i) % 4) * 4 + (zl + 4 - q) % 4
        fx(i, q, (x + i) % 4, slot).wait_recv()
        unpack(slot)
        return 0

    lax.fori_loop(0, 12, arrive, 0)
    stored.wait()
    sc = jnp.zeros((128, 64), F32)
    for a in range(16):
        feat = jnp.concatenate(
            [Ff[half, pl.ds(a, 64, stride=16), :] for half in range(2)], axis=1
        ).astype(BF)
        sc = sc + lax.dot_general(
            S[:, a * RANK : (a + 1) * RANK], feat, (((1,), (1,)), ((), ())), preferred_element_type=F32
        )
    rows = sc.reshape(8, 2, 8, 64)
    for cc in range(2):
        Sout[cc, :, :, pl.ds(0, 64)] = rows[:, cc]
    qh = rcopy(Sout.at[1 - c], Qh, s_qh, r_qh, sib)
    qh.start()
    for i in range(1, 4):
        fz(i, (zl + i) % 4, T).wait_send()
        for q in range(4):
            fx(i, q, (x + i) % 4, T).wait_send()
    qh.wait_recv()
    Sc[...] = Sout[c] + Qh[...]

    def q_copy(i, m, slot):
        return rcopy(Sc.at[m], Q.at[slot], s_q.at[i], r_q.at[slot], (T, m * 2 + c))

    def q_out(i, _):
        q_copy(i, peer(i, 1), me).start()
        return 0

    lax.fori_loop(0, 7, q_out, 0)
    qh.wait_send()

    def q_in(i, total):
        m = peer(6 - i, -1)
        q_copy(0, m, m).wait_recv()
        return total + Q[m]

    total = lax.fori_loop(0, 7, q_in, Sc[me])
    out_ref[...] = total[:, :64]
    lax.fori_loop(0, 7, lambda i, _: (q_copy(i, me, me).wait_send(), 0)[1], 0)


def local(
    activations, output_grads, turn_ids, turn_counts, input_basis, output_basis, stored_grads
):
    dma = pltpu.SemaphoreType.DMA
    hbm = pl.BlockSpec(memory_space=pl.ANY)
    out = pl.pallas_call(
        kernel,
        out_shape=jax.ShapeDtypeStruct((8, 64), F32),
        in_specs=[
            pl.BlockSpec(memory_space=pltpu.VMEM),
            pl.BlockSpec(memory_space=pltpu.SMEM),
            hbm,
            hbm,
            hbm,
            hbm,
            hbm,
        ],
        out_specs=pl.BlockSpec(memory_space=pltpu.VMEM),
        scratch_shapes=[
            pltpu.VMEM((2, TOK, D), BF),
            pltpu.VMEM((2, 16, 2, PC, RANK), BF),
            pltpu.VMEM((128, 4096), BF),
            pltpu.VMEM((2, TOKP, RANK), F32),
            pltpu.VMEM((1, TOKP), jnp.int32),
            pltpu.VMEM((2, 128, TOKP), F32),
            pltpu.VMEM((8, 64, RANK), F32),
            pltpu.VMEM((8, 64, RANK), BF),
            pltpu.VMEM((8, 64, RANK), BF),
            pltpu.VMEM((8, 64, RANK), BF),
            pltpu.VMEM((8, 64, RANK), BF),
            pltpu.VMEM((16, 64, RANK), BF),
            pltpu.VMEM((2, 1024, 128), F32),
            pltpu.VMEM((2, 8, 8, 128), F32),
            pltpu.VMEM((8, 8, 128), F32),
            pltpu.VMEM((8, 8, 128), F32),
            pltpu.VMEM((8, 8, 128), F32),
            dma((8,)),
            dma((4,)),
            dma,
            dma((64 * NS,)),
            dma((64,)),
            dma((32,)),
            dma((SEND_MAX,)),
            dma((4 * NS,)),
            dma,
            dma,
            dma((8,)),
            dma((8,)),
            dma((4,)),
            dma((16,)),
            dma((16,)),
            dma,
            dma,
            dma((8,)),
            dma((8,)),
        ],
        compiler_params=pltpu.CompilerParams(
            collective_id=0, has_side_effects=True, vmem_limit_bytes=60 * 1024 * 1024
        ),
        cost_estimate=pl.CostEstimate(
            flops=2 * 1460000000, bytes_accessed=12 * 1024 * 1024, transcendentals=0
        ),
    )(
        turn_ids,
        turn_counts,
        activations,
        output_grads,
        input_basis,
        output_basis,
        stored_grads,
    )
    return out.T


def solution(mesh):
    placed = (
        P(("turn", "tok"), None),
        P(("turn", "tok"), None),
        P(("turn", "tok")),
        P("turn"),
        P("tok", None),
        P("tok", None),
        P("turn", "tok"),
    )
    return jax.shard_map(
        local, mesh=mesh, in_specs=placed, out_specs=P(None, ("turn", "tok")), check_vma=False
    )
```

```python
import functools

import jax
import jax.numpy as jnp
from jax import lax
from jax.experimental import pallas as pl
from jax.experimental.pallas import tpu as pltpu
from jax.sharding import PartitionSpec as P

TURN_G = 4
TOK = 320
TOKP = 384
D = 8192
RANK = 256
CH = 512
PC = 256
NS = 2
ORDER = (
    8, 24, 9, 25, 4, 40, 56, 5, 10, 41, 57, 16, 12, 17, 26, 48,
    36, 28, 13, 37, 14, 49, 29, 60, 20, 61, 44, 50, 21, 27, 43, 52,
    45, 53, 58, 46, 63, 15, 23, 6, 62, 19, 39, 42, 22, 54, 7, 38,
    11, 30, 51, 59, 31, 18, 47, 55,
)
HALVES = ((1, 0, 0), (3, 0, 0), (0, 1, 0), (2, 0, 0), (3, 1, 0), (1, 1, 0), (2, 1, 0), (0, 1, 1), (1, 0, 1), (3, 0, 1), (3, 1, 1), (2, 0, 1), (1, 1, 1), (2, 1, 1))
SEND_MAX = 4 * NS + 4 * NS + len(ORDER) * 2
LAG = 3
BF = jnp.bfloat16
F32 = jnp.float32
MESH = pl.DeviceIdType.MESH


def kernel(
    ids_ref,
    cnt_ref,
    act_hbm,
    og_hbm,
    ib_hbm,
    ob_hbm,
    sg_hbm,
    out_ref,
    A,
    B,
    S,
    acc,
    ids,
    OT,
    Gf,
    Gs,
    Hin,
    Pb,
    Rin,
    Fb,
    Ff,
    Sout,
    Qh,
    Sc,
    Q,
    s_act,
    s_own,
    s_sg,
    r_piece,
    r_sib,
    s_sib,
    s_fwd,
    s_out,
    s_h,
    r_h,
    s_rs,
    r_rs,
    s_fz,
    s_fx,
    r_f,
    s_qh,
    r_qh,
    s_q,
    r_q,
):
    T = lax.axis_index("turn")
    K = lax.axis_index("tok")
    x, zl = T // 4, T % 4
    y, h, c = K // 4, (K // 2) % 2, K % 2
    z = h * 4 + zl
    edge = (zl == 0) | (zl == 3)
    inner = ((zl + 1) // 2) % 2
    p = (x + inner) % 2
    def tok_of(yy, hh, cc):
        return yy * 4 + hh * 2 + cc

    def zdev(zz):
        return ((x * 4 + zz % 4), tok_of(y, zz // 4, c))

    sib = (T, K + 1 - 2 * c)
    xs = {d: (((x + d + 4) % 4) * 4 + zl, K) for d in (1, -1)}
    ys = {d: (T, tok_of((y + d + 4) % 4, h, c)) for d in (1, -1)}
    me = y * 2 + h
    pair = (x * 4 + zl + 1 - 2 * (zl % 2), K)
    up = jnp.where(zl >= 2, 1, 7)
    over1 = zdev((z + up) % 8)
    over2 = zdev((z + up * 2) % 8)

    def rcopy(src, dst, ss, rs, dev):
        return pltpu.make_async_remote_copy(
            src_ref=src, dst_ref=dst, send_sem=ss, recv_sem=rs, device_id=dev, device_id_type=MESH
        )

    RB = TOK // 4
    R = PC // NS
    loads = []
    for b, hbm in enumerate((act_hbm, og_hbm)):
        for i in range(4):
            loads.append(
                pltpu.make_async_copy(
                    hbm.at[pl.ds(i * RB, RB)], A.at[b, pl.ds(i * RB, RB)], s_act.at[b * 4 + i]
                )
            )
    halves = (p, 1 - p)
    own = []
    for b, hbm in enumerate((ib_hbm, ob_hbm)):
        for half in range(2):
            rows = pl.ds(pl.multiple_of(halves[half] * PC, PC), PC)
            own.append(
                pltpu.make_async_copy(
                    hbm.at[rows], B.at[0, b, 0, 0, half], s_own.at[b * 2 + half]
                )
            )
    stored = pltpu.make_async_copy(sg_hbm, S, s_sg)
    for cp in own:
        cp.start()
    for cp in loads:
        cp.start()
    stored.start()

    barrier = pltpu.get_barrier_semaphore()

    def greet(dev):
        pl.semaphore_signal(barrier, inc=1, device_id=dev, device_id_type=MESH)

    greet(sib)
    greet(over2)
    for i in range(1, 4):
        greet((((x + i) % 4) * 4 + zl, K))
        greet((x * 4 + (zl + i) % 4, K))
    for i in range(1, 8):
        greet((T, ((me + i) % 8) * 2 + c))

    @pl.when(edge)
    def _():
        pl.semaphore_signal(barrier, inc=1, device_id=over1, device_id_type=MESH)

    acc[...] = jnp.zeros_like(acc)
    ids[...] = jnp.full_like(ids, -1)
    ids[0, pl.ds(0, TOK)] = ids_ref[...]
    Sout[...] = jnp.zeros_like(Sout)
    for cp in own:
        cp.wait()

    @pl.when(edge)
    def _():
        pl.semaphore_wait(barrier, 16)

    @pl.when(jnp.logical_not(edge))
    def _():
        pl.semaphore_wait(barrier, 15)

    def part(key, i):
        b, dy, dh, half = key
        code = (((b * 4 + dy) * 2 + dh) * 2 + half) * NS + i
        return B.at[0, b, dy, dh, half, pl.ds(i * R, R)], r_piece.at[code]

    sent = []

    def hand_on(key, i, dev, there):
        cp = rcopy(part(key, i)[0], part(there, i)[0], s_fwd.at[len(sent)], part(there, i)[1], dev)
        cp.start()
        sent.append(cp)

    def to_y(key, i, d):
        b, dy, dh, half = key
        hand_on(key, i, ys[d], (b, (dy - d) % 4, dh, half))

    def to_x(key, i, d):
        b, dy, dh, half = key
        hand_on(key, i, xs[d], (b, dy, dh, 1 - half))

    def to_pair(key, i):
        b, dy, dh, half = key
        hand_on(key, i, pair, (b, dy, dh, 1 - half))

    def boundary():
        out = []
        for b in range(2):
            for i in range(NS):
                for far, dev in enumerate((over1, over2)):
                    ref, rs = part((b, 0, 1, 0), i)
                    src = part((b, 0, 0, far), i)[0]
                    out.append(rcopy(src, ref, s_out.at[(b * NS + i) * 2 + far], rs, dev))
        return out

    for b in range(2):
        for i in range(NS):
            to_y((b, 0, 0, 0), i, 1)
            to_y((b, 0, 0, 0), i, -1)
            if b == 0 and i == 0:

                @pl.when(edge)
                def _():
                    for cp in boundary():
                        cp.start()

    shared = []

    def share_copy(key, n):
        b, dy, dh, half = key
        at = (b, dy, dh) if half is None else (b, dy, dh, half)
        rs = r_sib.at[((b * 4 + dy) * 2 + dh) * 2 + (half or 0)]
        return rcopy(B.at[(0,) + at], B.at[(1,) + at], s_sib.at[n], rs, sib)

    def share(key):
        cp = share_copy(key, len(shared))
        cp.start()
        shared.append(cp)

    for b in range(2):
        share((b, 0, 0, None))

    chunk = {
        (dy, dh): tok_of((y + dy) % 4, h if dh == 0 else 1 - h, 0) for dy in range(4) for dh in range(2)
    }

    def dots(b, blocks):
        lhs, rhs = [], []
        for core, dy, dh, half in blocks:
            kk = chunk[dy, dh] + (c if core == 0 else 1 - c)
            col = pl.multiple_of(kk * CH + halves[half] * PC, PC)
            lhs.append(A[b, :, pl.ds(col, PC)])
            rhs.append(B[core, b, dy, dh, half])
        acc[b, pl.ds(0, TOK)] += jnp.dot(
            jnp.concatenate(lhs, axis=1), jnp.concatenate(rhs, axis=0), preferred_element_type=F32
        )

    def dots_of(b, group):
        if group == 0:
            for cp in loads[4 * b : 4 * b + 4]:
                cp.wait()
            share_copy((b, 0, 0, None), 0).wait_recv()
            dots(b, [(core, 0, 0, half) for core in range(2) for half in range(2)])
            return
        keys = HALVES[2 * group - 2 : 2 * group]
        blocks = [(0,) + q for q in keys]
        if group == 7:
            dots(b, blocks)
            blocks = []
        for q in keys:
            share_copy((b,) + q, 0).wait_recv()
        dots(b, blocks + [(1,) + q for q in keys])

    events = []
    for code in ORDER:
        i, half, dh, dy, b = code % NS, code // NS % 2, code // NS // 2 % 2, code // NS // 4 % 4, code // NS // 16
        events.append(((b, dy, dh, half), i))
    last = {key: n for n, (key, i) in enumerate(events)}
    due = []
    for b in range(2):
        due.append((NS + NS * b, b, 0))
        for group in range(1, 8):
            n = max(last[(b,) + q] for q in HALVES[2 * group - 2 : 2 * group])
            due.append((n + LAG, b, group))
    due.sort(key=lambda e: (e[0], e[2]))

    for n, (key, i) in enumerate(events):
        b, dy, dh, half = key
        ref, rs = part(key, i)
        rcopy(ref, ref, s_fwd.at[0], rs, sib).wait_recv()
        if half == 0 and dy == 0:
            to_y(key, i, 1)
            to_y(key, i, -1)
            to_pair(key, i)
        elif half == 0:
            side = {3: 0, 1: 1, 2: b if dh == 0 else 1 - b}[dy]
            d = 1 if side == 0 else -1
            if dy != 2 and (b == side) == (dh == 0):
                to_y(key, i, d)
            to_x(key, i, d)
        if last[key] == n:
            share(key)
        while due and due[0][0] <= n:
            _, bb, group = due.pop(0)
            dots_of(bb, group)
    for _, bb, group in due:
        dots_of(bb, group)

    in_c = acc[0].astype(BF)
    out_t = acc[1].T.reshape(8, 2, 16, TOKP)
    for cc in range(2):
        OT[cc] = out_t[:, cc].reshape(128, TOKP)
    local = ids[...] - T * TURN_G

    def gradient(cc, t):
        lhs = jnp.where(local == t, OT[cc], 0.0).astype(BF)
        return jnp.dot(lhs, in_c, preferred_element_type=F32).reshape(8, 16, RANK)

    for t in range(TURN_G):
        Gs[:, pl.ds(t * 16, 16), :] = gradient(1 - c, t).astype(BF)
    hc = rcopy(Gs, Hin, s_h, r_h, sib)
    hc.start()
    for t in range(TURN_G):
        Gf[:, pl.ds(t * 16, 16), :] = gradient(c, t)
    hc.wait_recv()

    def peer(i, sign):
        far = i < 4
        yy = (y + 4 + sign * jnp.where(far, i, i - 3)) % 4
        return yy * 2 + jnp.where(far, 1 - h, h)

    def rs_copy(i, m, slot):
        return rcopy(Pb.at[m], Rin.at[slot], s_rs.at[i], r_rs.at[slot], (T, m * 2 + c))

    def rs_out(i, _):
        m = peer(i, 1)
        Pb[m] = (Gf[m] + Hin[m].astype(F32)).astype(BF)
        rs_copy(i, m, me).start()
        return 0

    lax.fori_loop(0, 7, rs_out, 0)
    Gf[me] = Gf[me] + Hin[me].astype(F32)
    for cp in sent + shared:
        cp.wait_send()

    @pl.when(edge)
    def _():
        for cp in boundary():
            cp.wait_send()

    hc.wait_send()

    def rs_in(i, _):
        m = peer(6 - i, -1)
        rs_copy(0, m, m).wait_recv()
        Gf[me] = Gf[me] + Rin[m].astype(F32)
        return 0

    lax.fori_loop(0, 7, rs_in, 0)
    for t in range(TURN_G):
        n = cnt_ref[t].astype(F32)
        rows = pl.ds(t * 16, 16)
        Fb[T, rows] = (Gf[me, rows] / n).astype(BF)

    def fz(i, zz, slot):
        return rcopy(Fb.at[slot], Fb.at[slot], s_fz.at[i], r_f.at[slot], (x * 4 + zz, K))

    def fx(i, q, xx, slot):
        return rcopy(
            Fb.at[slot], Fb.at[slot], s_fx.at[q * 4 + i], r_f.at[slot], (xx * 4 + zl, K)
        )

    def unpack(slot):
        rows = pl.ds(pl.multiple_of(slot * 64, 64), 64)
        for half in range(2):
            Ff[half, rows] = Fb[slot, :, half * 128 : (half + 1) * 128].astype(F32)

    for i in range(1, 4):
        fz(i, (zl + i) % 4, T).start()
    for i in range(1, 4):
        fx(i, 0, (x + i) % 4, T).start()
    unpack(T)
    lax.fori_loop(0, 7, lambda i, _: (rs_copy(i, me, me).wait_send(), 0)[1], 0)

    def hand(q, _):
        zz = (zl + 4 - q) % 4
        slot = x * 4 + zz
        fz(q, zz, slot).wait_recv()
        for i in range(1, 4):
            fx(i, q, (x + i) % 4, slot).start()
        unpack(slot)
        return 0

    lax.fori_loop(1, 4, hand, 0)

    def arrive(n, _):
        q, i = n // 3, n % 3 + 1
        slot = ((x + 4 - i) % 4) * 4 + (zl + 4 - q) % 4
        fx(i, q, (x + i) % 4, slot).wait_recv()
        unpack(slot)
        return 0

    lax.fori_loop(0, 12, arrive, 0)
    stored.wait()
    sc = jnp.zeros((128, 64), F32)
    for a in range(16):
        feat = jnp.concatenate(
            [Ff[half, pl.ds(a, 64, stride=16), :] for half in range(2)], axis=1
        ).astype(BF)
        sc = sc + lax.dot_general(
            S[:, a * RANK : (a + 1) * RANK], feat, (((1,), (1,)), ((), ())), preferred_element_type=F32
        )
    rows = sc.reshape(8, 2, 8, 64)
    for cc in range(2):
        Sout[cc, :, :, pl.ds(0, 64)] = rows[:, cc]
    qh = rcopy(Sout.at[1 - c], Qh, s_qh, r_qh, sib)
    qh.start()
    for i in range(1, 4):
        fz(i, (zl + i) % 4, T).wait_send()
        for q in range(4):
            fx(i, q, (x + i) % 4, T).wait_send()
    qh.wait_recv()
    Sc[...] = Sout[c] + Qh[...]

    def q_copy(i, m, slot):
        return rcopy(Sc.at[m], Q.at[slot], s_q.at[i], r_q.at[slot], (T, m * 2 + c))

    def q_out(i, _):
        q_copy(i, peer(i, 1), me).start()
        return 0

    lax.fori_loop(0, 7, q_out, 0)
    qh.wait_send()

    def q_in(i, total):
        m = peer(6 - i, -1)
        q_copy(0, m, m).wait_recv()
        return total + Q[m]

    total = lax.fori_loop(0, 7, q_in, Sc[me])
    out_ref[...] = total[:, :64]
    lax.fori_loop(0, 7, lambda i, _: (q_copy(i, me, me).wait_send(), 0)[1], 0)


def local(
    activations, output_grads, turn_ids, turn_counts, input_basis, output_basis, stored_grads
):
    dma = pltpu.SemaphoreType.DMA
    hbm = pl.BlockSpec(memory_space=pl.ANY)
    out = pl.pallas_call(
        kernel,
        out_shape=jax.ShapeDtypeStruct((8, 64), F32),
        in_specs=[
            pl.BlockSpec(memory_space=pltpu.VMEM),
            pl.BlockSpec(memory_space=pltpu.SMEM),
            hbm,
            hbm,
            hbm,
            hbm,
            hbm,
        ],
        out_specs=pl.BlockSpec(memory_space=pltpu.VMEM),
        scratch_shapes=[
            pltpu.VMEM((2, TOK, D), BF),
            pltpu.VMEM((2, 2, 4, 2, 2, PC, RANK), BF),
            pltpu.VMEM((128, 4096), BF),
            pltpu.VMEM((2, TOKP, RANK), F32),
            pltpu.VMEM((1, TOKP), jnp.int32),
            pltpu.VMEM((2, 128, TOKP), F32),
            pltpu.VMEM((8, 64, RANK), F32),
            pltpu.VMEM((8, 64, RANK), BF),
            pltpu.VMEM((8, 64, RANK), BF),
            pltpu.VMEM((8, 64, RANK), BF),
            pltpu.VMEM((8, 64, RANK), BF),
            pltpu.VMEM((16, 64, RANK), BF),
            pltpu.VMEM((2, 1024, 128), F32),
            pltpu.VMEM((2, 8, 8, 128), F32),
            pltpu.VMEM((8, 8, 128), F32),
            pltpu.VMEM((8, 8, 128), F32),
            pltpu.VMEM((8, 8, 128), F32),
            dma((8,)),
            dma((4,)),
            dma,
            dma((32 * NS,)),
            dma((32,)),
            dma((32,)),
            dma((SEND_MAX,)),
            dma((4 * NS,)),
            dma,
            dma,
            dma((8,)),
            dma((8,)),
            dma((4,)),
            dma((16,)),
            dma((16,)),
            dma,
            dma,
            dma((8,)),
            dma((8,)),
        ],
        compiler_params=pltpu.CompilerParams(
            collective_id=0, has_side_effects=True, vmem_limit_bytes=60 * 1024 * 1024
        ),
        cost_estimate=pl.CostEstimate(
            flops=2 * 1460000000, bytes_accessed=12 * 1024 * 1024, transcendentals=0
        ),
    )(
        turn_ids,
        turn_counts,
        activations,
        output_grads,
        input_basis,
        output_basis,
        stored_grads,
    )
    return out.T


def solution(mesh):
    placed = (
        P(("turn", "tok"), None),
        P(("turn", "tok"), None),
        P(("turn", "tok")),
        P("turn"),
        P("tok", None),
        P("tok", None),
        P("turn", "tok"),
    )
    return jax.shard_map(
        local, mesh=mesh, in_specs=placed, out_specs=P(None, ("turn", "tok")), check_vma=False
    )
```

```python
import functools

import jax
import jax.numpy as jnp
from jax import lax
from jax.experimental import pallas as pl
from jax.experimental.pallas import tpu as pltpu
from jax.sharding import PartitionSpec as P

TURN_G = 4
TOK = 320
TOKP = 384
D = 8192
RANK = 256
CH = 512
PC = 256
NS = 2
ORDER = (
    8, 24, 9, 25, 4, 40, 56, 5, 10, 41, 57, 16, 12, 17, 26, 48,
    36, 28, 13, 37, 14, 49, 29, 60, 20, 61, 44, 50, 21, 27, 43, 52,
    45, 53, 58, 46, 63, 15, 23, 6, 62, 19, 39, 42, 22, 54, 7, 38,
    11, 30, 51, 59, 31, 18, 47, 55,
)
SEND_MAX = 4 * NS + 4 * NS + len(ORDER) * 2
LAG = 13
FIRST = 16
BF = jnp.bfloat16
F32 = jnp.float32
MESH = pl.DeviceIdType.MESH


def kernel(
    ids_ref,
    cnt_ref,
    act_hbm,
    og_hbm,
    ib_hbm,
    ob_hbm,
    sg_hbm,
    out_ref,
    A,
    B,
    S,
    acc,
    ids,
    OT,
    Gf,
    Gs,
    Hin,
    Pb,
    Rin,
    Fb,
    Ff,
    Sout,
    Qh,
    Sc,
    Q,
    s_act,
    s_own,
    s_sg,
    r_piece,
    r_sib,
    s_sib,
    s_fwd,
    s_out,
    s_h,
    r_h,
    s_rs,
    r_rs,
    s_fz,
    s_fx,
    r_f,
    s_qh,
    r_qh,
    s_q,
    r_q,
):
    T = lax.axis_index("turn")
    K = lax.axis_index("tok")
    x, zl = T // 4, T % 4
    y, h, c = K // 4, (K // 2) % 2, K % 2
    z = h * 4 + zl
    edge = (zl == 0) | (zl == 3)
    inner = ((zl + 1) // 2) % 2
    p = (x + inner) % 2
    def tok_of(yy, hh, cc):
        return yy * 4 + hh * 2 + cc

    def zdev(zz):
        return ((x * 4 + zz % 4), tok_of(y, zz // 4, c))

    sib = (T, K + 1 - 2 * c)
    xs = {d: (((x + d + 4) % 4) * 4 + zl, K) for d in (1, -1)}
    ys = {d: (T, tok_of((y + d + 4) % 4, h, c)) for d in (1, -1)}
    me = y * 2 + h
    pair = (x * 4 + zl + 1 - 2 * (zl % 2), K)
    up = jnp.where(zl >= 2, 1, 7)
    over1 = zdev((z + up) % 8)
    over2 = zdev((z + up * 2) % 8)

    def rcopy(src, dst, ss, rs, dev):
        return pltpu.make_async_remote_copy(
            src_ref=src, dst_ref=dst, send_sem=ss, recv_sem=rs, device_id=dev, device_id_type=MESH
        )

    RB = TOK // 4
    R = PC // NS
    loads = []
    for b, hbm in enumerate((act_hbm, og_hbm)):
        for i in range(4):
            loads.append(
                pltpu.make_async_copy(
                    hbm.at[pl.ds(i * RB, RB)], A.at[b, pl.ds(i * RB, RB)], s_act.at[b * 4 + i]
                )
            )
    halves = (p, 1 - p)
    own = []
    for b, hbm in enumerate((ib_hbm, ob_hbm)):
        for half in range(2):
            rows = pl.ds(pl.multiple_of(halves[half] * PC, PC), PC)
            own.append(
                pltpu.make_async_copy(
                    hbm.at[rows], B.at[0, b, 0, 0, half], s_own.at[b * 2 + half]
                )
            )
    stored = pltpu.make_async_copy(sg_hbm, S, s_sg)
    for cp in own:
        cp.start()
    for cp in loads:
        cp.start()
    stored.start()

    barrier = pltpu.get_barrier_semaphore()

    def greet(dev):
        pl.semaphore_signal(barrier, inc=1, device_id=dev, device_id_type=MESH)

    greet(sib)
    greet(over2)
    for i in range(1, 4):
        greet((((x + i) % 4) * 4 + zl, K))
        greet((x * 4 + (zl + i) % 4, K))
    for i in range(1, 8):
        greet((T, ((me + i) % 8) * 2 + c))

    @pl.when(edge)
    def _():
        pl.semaphore_signal(barrier, inc=1, device_id=over1, device_id_type=MESH)

    acc[...] = jnp.zeros_like(acc)
    ids[...] = jnp.full_like(ids, -1)
    ids[0, pl.ds(0, TOK)] = ids_ref[...]
    Sout[...] = jnp.zeros_like(Sout)
    for cp in own:
        cp.wait()

    @pl.when(edge)
    def _():
        pl.semaphore_wait(barrier, 16)

    @pl.when(jnp.logical_not(edge))
    def _():
        pl.semaphore_wait(barrier, 15)

    def part(key, i):
        b, dy, dh, half = key
        code = (((b * 4 + dy) * 2 + dh) * 2 + half) * NS + i
        return B.at[0, b, dy, dh, half, pl.ds(i * R, R)], r_piece.at[code]

    sent = []

    def hand_on(key, i, dev, there):
        cp = rcopy(part(key, i)[0], part(there, i)[0], s_fwd.at[len(sent)], part(there, i)[1], dev)
        cp.start()
        sent.append(cp)

    def to_y(key, i, d):
        b, dy, dh, half = key
        hand_on(key, i, ys[d], (b, (dy - d) % 4, dh, half))

    def to_x(key, i, d):
        b, dy, dh, half = key
        hand_on(key, i, xs[d], (b, dy, dh, 1 - half))

    def to_pair(key, i):
        b, dy, dh, half = key
        hand_on(key, i, pair, (b, dy, dh, 1 - half))

    def boundary():
        out = []
        for b in range(2):
            for i in range(NS):
                for far, dev in enumerate((over1, over2)):
                    ref, rs = part((b, 0, 1, 0), i)
                    src = part((b, 0, 0, far), i)[0]
                    out.append(rcopy(src, ref, s_out.at[(b * NS + i) * 2 + far], rs, dev))
        return out

    for b in range(2):
        for i in range(NS):
            to_y((b, 0, 0, 0), i, 1)
            to_y((b, 0, 0, 0), i, -1)
            if b == 0 and i == 0:

                @pl.when(edge)
                def _():
                    for cp in boundary():
                        cp.start()

    shared = []

    def share_copy(key, n):
        b, dy, dh, half = key
        at = (b, dy, dh) if half is None else (b, dy, dh, half)
        rs = r_sib.at[((b * 4 + dy) * 2 + dh) * 2 + (half or 0)]
        return rcopy(B.at[(0,) + at], B.at[(1,) + at], s_sib.at[n], rs, sib)

    def share(key):
        cp = share_copy(key, len(shared))
        cp.start()
        shared.append(cp)

    for b in range(2):
        share((b, 0, 0, None))

    chunk = {
        (dy, dh): tok_of((y + dy) % 4, h if dh == 0 else 1 - h, 0) for dy in range(4) for dh in range(2)
    }

    def dots(b, blocks):
        lhs, rhs = [], []
        for core, dy, dh, half in blocks:
            kk = chunk[dy, dh] + (c if core == 0 else 1 - c)
            col = pl.multiple_of(kk * CH + halves[half] * PC, PC)
            lhs.append(A[b, :, pl.ds(col, PC)])
            rhs.append(B[core, b, dy, dh, half])
        acc[b, pl.ds(0, TOK)] += jnp.dot(
            jnp.concatenate(lhs, axis=1), jnp.concatenate(rhs, axis=0), preferred_element_type=F32
        )

    def dots_of(b, group):
        if group == 0:
            for cp in loads[4 * b : 4 * b + 4]:
                cp.wait()
            share_copy((b, 0, 0, None), 0).wait_recv()
            dots(b, [(core, 0, 0, half) for core in range(2) for half in range(2)])
            return
        keys = done[b][2 * group - 2 : 2 * group]
        blocks = [(0,) + q for q in keys]
        if group == 7:
            dots(b, blocks)
            blocks = []
        for q in keys:
            share_copy((b,) + q, 0).wait_recv()
        dots(b, blocks + [(1,) + q for q in keys])

    events = []
    for code in ORDER:
        i, half, dh, dy, b = code % NS, code // NS % 2, code // NS // 2 % 2, code // NS // 4 % 4, code // NS // 16
        events.append(((b, dy, dh, half), i))
    last = {key: n for n, (key, i) in enumerate(events)}
    done = [sorted((k[1:] for k in last if k[0] == b), key=lambda q: last[(b,) + q]) for b in range(2)]
    due = []
    for b in range(2):
        due.append((FIRST, b, 0))
        for group in range(1, 8):
            n = max(last[(b,) + q] for q in done[b][2 * group - 2 : 2 * group])
            due.append((max(n + LAG, FIRST), b, group))
    due.sort(key=lambda e: (e[0], e[2]))

    for n, (key, i) in enumerate(events):
        b, dy, dh, half = key
        ref, rs = part(key, i)
        rcopy(ref, ref, s_fwd.at[0], rs, sib).wait_recv()
        if half == 0 and dy == 0:
            to_y(key, i, 1)
            to_y(key, i, -1)
            to_pair(key, i)
        elif half == 0:
            side = {3: 0, 1: 1, 2: b if dh == 0 else 1 - b}[dy]
            d = 1 if side == 0 else -1
            if dy != 2 and (b == side) == (dh == 0):
                to_y(key, i, d)
            to_x(key, i, d)
        if last[key] == n:
            share(key)
        if due and due[0][0] <= n:
            _, bb, group = due.pop(0)
            dots_of(bb, group)
    for _, bb, group in due:
        dots_of(bb, group)

    in_c = acc[0].astype(BF)
    out_t = acc[1].T.reshape(8, 2, 16, TOKP)
    for cc in range(2):
        OT[cc] = out_t[:, cc].reshape(128, TOKP)
    local = ids[...] - T * TURN_G

    def gradient(cc, t):
        lhs = jnp.where(local == t, OT[cc], 0.0).astype(BF)
        return jnp.dot(lhs, in_c, preferred_element_type=F32).reshape(8, 16, RANK)

    for t in range(TURN_G):
        Gs[:, pl.ds(t * 16, 16), :] = gradient(1 - c, t).astype(BF)
    hc = rcopy(Gs, Hin, s_h, r_h, sib)
    hc.start()
    for t in range(TURN_G):
        Gf[:, pl.ds(t * 16, 16), :] = gradient(c, t)
    hc.wait_recv()

    def peer(i, sign):
        far = i < 4
        yy = (y + 4 + sign * jnp.where(far, i, i - 3)) % 4
        return yy * 2 + jnp.where(far, 1 - h, h)

    def rs_copy(i, m, slot):
        return rcopy(Pb.at[m], Rin.at[slot], s_rs.at[i], r_rs.at[slot], (T, m * 2 + c))

    def rs_out(i, _):
        m = peer(i, 1)
        Pb[m] = (Gf[m] + Hin[m].astype(F32)).astype(BF)
        rs_copy(i, m, me).start()
        return 0

    lax.fori_loop(0, 7, rs_out, 0)
    Gf[me] = Gf[me] + Hin[me].astype(F32)
    for cp in sent + shared:
        cp.wait_send()

    @pl.when(edge)
    def _():
        for cp in boundary():
            cp.wait_send()

    hc.wait_send()

    def rs_in(i, _):
        m = peer(6 - i, -1)
        rs_copy(0, m, m).wait_recv()
        Gf[me] = Gf[me] + Rin[m].astype(F32)
        return 0

    lax.fori_loop(0, 7, rs_in, 0)
    for t in range(TURN_G):
        n = cnt_ref[t].astype(F32)
        rows = pl.ds(t * 16, 16)
        Fb[T, rows] = (Gf[me, rows] / n).astype(BF)

    def fz(i, zz, slot):
        return rcopy(Fb.at[slot], Fb.at[slot], s_fz.at[i], r_f.at[slot], (x * 4 + zz, K))

    def fx(i, q, xx, slot):
        return rcopy(
            Fb.at[slot], Fb.at[slot], s_fx.at[q * 4 + i], r_f.at[slot], (xx * 4 + zl, K)
        )

    def unpack(slot):
        rows = pl.ds(pl.multiple_of(slot * 64, 64), 64)
        for half in range(2):
            Ff[half, rows] = Fb[slot, :, half * 128 : (half + 1) * 128].astype(F32)

    for i in range(1, 4):
        fz(i, (zl + i) % 4, T).start()
    for i in range(1, 4):
        fx(i, 0, (x + i) % 4, T).start()
    unpack(T)
    lax.fori_loop(0, 7, lambda i, _: (rs_copy(i, me, me).wait_send(), 0)[1], 0)

    def hand(q, _):
        zz = (zl + 4 - q) % 4
        slot = x * 4 + zz
        fz(q, zz, slot).wait_recv()
        for i in range(1, 4):
            fx(i, q, (x + i) % 4, slot).start()
        unpack(slot)
        return 0

    lax.fori_loop(1, 4, hand, 0)

    def arrive(n, _):
        q, i = n // 3, n % 3 + 1
        slot = ((x + 4 - i) % 4) * 4 + (zl + 4 - q) % 4
        fx(i, q, (x + i) % 4, slot).wait_recv()
        unpack(slot)
        return 0

    lax.fori_loop(0, 12, arrive, 0)
    stored.wait()
    sc = jnp.zeros((128, 64), F32)
    for a in range(16):
        feat = jnp.concatenate(
            [Ff[half, pl.ds(a, 64, stride=16), :] for half in range(2)], axis=1
        ).astype(BF)
        sc = sc + lax.dot_general(
            S[:, a * RANK : (a + 1) * RANK], feat, (((1,), (1,)), ((), ())), preferred_element_type=F32
        )
    rows = sc.reshape(8, 2, 8, 64)
    for cc in range(2):
        Sout[cc, :, :, pl.ds(0, 64)] = rows[:, cc]
    qh = rcopy(Sout.at[1 - c], Qh, s_qh, r_qh, sib)
    qh.start()
    for i in range(1, 4):
        fz(i, (zl + i) % 4, T).wait_send()
        for q in range(4):
            fx(i, q, (x + i) % 4, T).wait_send()
    qh.wait_recv()
    Sc[...] = Sout[c] + Qh[...]

    def q_copy(i, m, slot):
        return rcopy(Sc.at[m], Q.at[slot], s_q.at[i], r_q.at[slot], (T, m * 2 + c))

    def q_out(i, _):
        q_copy(i, peer(i, 1), me).start()
        return 0

    lax.fori_loop(0, 7, q_out, 0)
    qh.wait_send()

    def q_in(i, total):
        m = peer(6 - i, -1)
        q_copy(0, m, m).wait_recv()
        return total + Q[m]

    total = lax.fori_loop(0, 7, q_in, Sc[me])
    out_ref[...] = total[:, :64]
    lax.fori_loop(0, 7, lambda i, _: (q_copy(i, me, me).wait_send(), 0)[1], 0)


def local(
    activations, output_grads, turn_ids, turn_counts, input_basis, output_basis, stored_grads
):
    dma = pltpu.SemaphoreType.DMA
    hbm = pl.BlockSpec(memory_space=pl.ANY)
    out = pl.pallas_call(
        kernel,
        out_shape=jax.ShapeDtypeStruct((8, 64), F32),
        in_specs=[
            pl.BlockSpec(memory_space=pltpu.VMEM),
            pl.BlockSpec(memory_space=pltpu.SMEM),
            hbm,
            hbm,
            hbm,
            hbm,
            hbm,
        ],
        out_specs=pl.BlockSpec(memory_space=pltpu.VMEM),
        scratch_shapes=[
            pltpu.VMEM((2, TOK, D), BF),
            pltpu.VMEM((2, 2, 4, 2, 2, PC, RANK), BF),
            pltpu.VMEM((128, 4096), BF),
            pltpu.VMEM((2, TOKP, RANK), F32),
            pltpu.VMEM((1, TOKP), jnp.int32),
            pltpu.VMEM((2, 128, TOKP), F32),
            pltpu.VMEM((8, 64, RANK), F32),
            pltpu.VMEM((8, 64, RANK), BF),
            pltpu.VMEM((8, 64, RANK), BF),
            pltpu.VMEM((8, 64, RANK), BF),
            pltpu.VMEM((8, 64, RANK), BF),
            pltpu.VMEM((16, 64, RANK), BF),
            pltpu.VMEM((2, 1024, 128), F32),
            pltpu.VMEM((2, 8, 8, 128), F32),
            pltpu.VMEM((8, 8, 128), F32),
            pltpu.VMEM((8, 8, 128), F32),
            pltpu.VMEM((8, 8, 128), F32),
            dma((8,)),
            dma((4,)),
            dma,
            dma((32 * NS,)),
            dma((32,)),
            dma((32,)),
            dma((SEND_MAX,)),
            dma((4 * NS,)),
            dma,
            dma,
            dma((8,)),
            dma((8,)),
            dma((4,)),
            dma((16,)),
            dma((16,)),
            dma,
            dma,
            dma((8,)),
            dma((8,)),
        ],
        compiler_params=pltpu.CompilerParams(
            collective_id=0, has_side_effects=True, vmem_limit_bytes=60 * 1024 * 1024
        ),
        cost_estimate=pl.CostEstimate(
            flops=2 * 1460000000, bytes_accessed=12 * 1024 * 1024, transcendentals=0
        ),
    )(
        turn_ids,
        turn_counts,
        activations,
        output_grads,
        input_basis,
        output_basis,
        stored_grads,
    )
    return out.T


def solution(mesh):
    placed = (
        P(("turn", "tok"), None),
        P(("turn", "tok"), None),
        P(("turn", "tok")),
        P("turn"),
        P("tok", None),
        P("tok", None),
        P("turn", "tok"),
    )
    return jax.shard_map(
        local, mesh=mesh, in_specs=placed, out_specs=P(None, ("turn", "tok")), check_vma=False
    )
```

```python
import functools

import jax
import jax.numpy as jnp
from jax import lax
from jax.experimental import pallas as pl
from jax.experimental.pallas import tpu as pltpu
from jax.sharding import PartitionSpec as P

TURN_G = 4
TOK = 320
TOKP = 384
D = 8192
RANK = 256
CH = 512
PC = 256
NS = 1
ORDER = (
    4, 12, 2, 28, 20, 8, 6, 18, 24, 3, 14, 30, 10, 22, 13, 29,
    21, 19, 26, 5, 25, 9, 15, 7, 31, 11, 23, 27,
)
SEND_MAX = 4 * NS + 4 * NS + len(ORDER) * 2
LAG = 7
FIRST = 8
BF = jnp.bfloat16
F32 = jnp.float32
MESH = pl.DeviceIdType.MESH


def kernel(
    ids_ref,
    cnt_ref,
    act_hbm,
    og_hbm,
    ib_hbm,
    ob_hbm,
    sg_hbm,
    out_ref,
    A,
    B,
    S,
    acc,
    ids,
    OT,
    Gf,
    Gs,
    Hin,
    Pb,
    Rin,
    Fb,
    Ff,
    Sout,
    Qh,
    Sc,
    Q,
    s_act,
    s_own,
    s_sg,
    r_piece,
    r_sib,
    s_sib,
    s_fwd,
    s_out,
    s_h,
    r_h,
    s_rs,
    r_rs,
    s_fz,
    s_fx,
    r_f,
    s_qh,
    r_qh,
    s_q,
    r_q,
):
    T = lax.axis_index("turn")
    K = lax.axis_index("tok")
    x, zl = T // 4, T % 4
    y, h, c = K // 4, (K // 2) % 2, K % 2
    z = h * 4 + zl
    edge = (zl == 0) | (zl == 3)
    inner = ((zl + 1) // 2) % 2
    p = (x + inner) % 2
    def tok_of(yy, hh, cc):
        return yy * 4 + hh * 2 + cc

    def zdev(zz):
        return ((x * 4 + zz % 4), tok_of(y, zz // 4, c))

    sib = (T, K + 1 - 2 * c)
    xs = {d: (((x + d + 4) % 4) * 4 + zl, K) for d in (1, -1)}
    ys = {d: (T, tok_of((y + d + 4) % 4, h, c)) for d in (1, -1)}
    me = y * 2 + h
    pair = (x * 4 + zl + 1 - 2 * (zl % 2), K)
    up = jnp.where(zl >= 2, 1, 7)
    over1 = zdev((z + up) % 8)
    over2 = zdev((z + up * 2) % 8)

    def rcopy(src, dst, ss, rs, dev):
        return pltpu.make_async_remote_copy(
            src_ref=src, dst_ref=dst, send_sem=ss, recv_sem=rs, device_id=dev, device_id_type=MESH
        )

    RB = TOK // 4
    R = PC // NS
    loads = []
    for b, hbm in enumerate((act_hbm, og_hbm)):
        for i in range(4):
            loads.append(
                pltpu.make_async_copy(
                    hbm.at[pl.ds(i * RB, RB)], A.at[b, pl.ds(i * RB, RB)], s_act.at[b * 4 + i]
                )
            )
    halves = (p, 1 - p)
    own = []
    for b, hbm in enumerate((ib_hbm, ob_hbm)):
        for half in range(2):
            rows = pl.ds(pl.multiple_of(halves[half] * PC, PC), PC)
            own.append(
                pltpu.make_async_copy(
                    hbm.at[rows], B.at[0, b, 0, 0, half], s_own.at[b * 2 + half]
                )
            )
    stored = pltpu.make_async_copy(sg_hbm, S, s_sg)
    for cp in own:
        cp.start()
    for cp in loads:
        cp.start()
    stored.start()

    barrier = pltpu.get_barrier_semaphore()

    def greet(dev):
        pl.semaphore_signal(barrier, inc=1, device_id=dev, device_id_type=MESH)

    greet(sib)
    greet(over2)
    for i in range(1, 4):
        greet((((x + i) % 4) * 4 + zl, K))
        greet((x * 4 + (zl + i) % 4, K))
    for i in range(1, 8):
        greet((T, ((me + i) % 8) * 2 + c))

    @pl.when(edge)
    def _():
        pl.semaphore_signal(barrier, inc=1, device_id=over1, device_id_type=MESH)

    acc[...] = jnp.zeros_like(acc)
    ids[...] = jnp.full_like(ids, -1)
    ids[0, pl.ds(0, TOK)] = ids_ref[...]
    Sout[...] = jnp.zeros_like(Sout)
    for cp in own:
        cp.wait()

    @pl.when(edge)
    def _():
        pl.semaphore_wait(barrier, 16)

    @pl.when(jnp.logical_not(edge))
    def _():
        pl.semaphore_wait(barrier, 15)

    def part(key, i):
        b, dy, dh, half = key
        code = (((b * 4 + dy) * 2 + dh) * 2 + half) * NS + i
        return B.at[0, b, dy, dh, half, pl.ds(i * R, R)], r_piece.at[code]

    sent = []

    def hand_on(key, i, dev, there):
        cp = rcopy(part(key, i)[0], part(there, i)[0], s_fwd.at[len(sent)], part(there, i)[1], dev)
        cp.start()
        sent.append(cp)

    def to_y(key, i, d):
        b, dy, dh, half = key
        hand_on(key, i, ys[d], (b, (dy - d) % 4, dh, half))

    def to_x(key, i, d):
        b, dy, dh, half = key
        hand_on(key, i, xs[d], (b, dy, dh, 1 - half))

    def to_pair(key, i):
        b, dy, dh, half = key
        hand_on(key, i, pair, (b, dy, dh, 1 - half))

    def boundary():
        out = []
        for b in range(2):
            for i in range(NS):
                for far, dev in enumerate((over1, over2)):
                    ref, rs = part((b, 0, 1, 0), i)
                    src = part((b, 0, 0, far), i)[0]
                    out.append(rcopy(src, ref, s_out.at[(b * NS + i) * 2 + far], rs, dev))
        return out

    for b in range(2):
        for i in range(NS):
            to_y((b, 0, 0, 0), i, 1)
            to_y((b, 0, 0, 0), i, -1)
            if b == 0 and i == 0:

                @pl.when(edge)
                def _():
                    for cp in boundary():
                        cp.start()

    shared = []

    def share_copy(key, n):
        b, dy, dh, half = key
        at = (b, dy, dh) if half is None else (b, dy, dh, half)
        rs = r_sib.at[((b * 4 + dy) * 2 + dh) * 2 + (half or 0)]
        return rcopy(B.at[(0,) + at], B.at[(1,) + at], s_sib.at[n], rs, sib)

    def share(key):
        cp = share_copy(key, len(shared))
        cp.start()
        shared.append(cp)

    for b in range(2):
        share((b, 0, 0, None))

    chunk = {
        (dy, dh): tok_of((y + dy) % 4, h if dh == 0 else 1 - h, 0) for dy in range(4) for dh in range(2)
    }

    def dots(b, blocks):
        lhs, rhs = [], []
        for core, dy, dh, half in blocks:
            kk = chunk[dy, dh] + (c if core == 0 else 1 - c)
            col = pl.multiple_of(kk * CH + halves[half] * PC, PC)
            lhs.append(A[b, :, pl.ds(col, PC)])
            rhs.append(B[core, b, dy, dh, half])
        acc[b, pl.ds(0, TOK)] += jnp.dot(
            jnp.concatenate(lhs, axis=1), jnp.concatenate(rhs, axis=0), preferred_element_type=F32
        )

    def dots_of(b, group):
        if group == 0:
            for cp in loads[4 * b : 4 * b + 4]:
                cp.wait()
            share_copy((b, 0, 0, None), 0).wait_recv()
            dots(b, [(core, 0, 0, half) for core in range(2) for half in range(2)])
            return
        keys = done[b][2 * group - 2 : 2 * group]
        blocks = [(0,) + q for q in keys]
        if group == 7:
            dots(b, blocks)
            blocks = []
        for q in keys:
            share_copy((b,) + q, 0).wait_recv()
        dots(b, blocks + [(1,) + q for q in keys])

    events = []
    for code in ORDER:
        i, half, dh, dy, b = code % NS, code // NS % 2, code // NS // 2 % 2, code // NS // 4 % 4, code // NS // 16
        events.append(((b, dy, dh, half), i))
    last = {key: n for n, (key, i) in enumerate(events)}
    done = [sorted((k[1:] for k in last if k[0] == b), key=lambda q: last[(b,) + q]) for b in range(2)]
    due = []
    for b in range(2):
        due.append((FIRST, b, 0))
        for group in range(1, 8):
            n = max(last[(b,) + q] for q in done[b][2 * group - 2 : 2 * group])
            due.append((max(n + LAG, FIRST), b, group))
    due.sort(key=lambda e: (e[0], e[2]))

    for n, (key, i) in enumerate(events):
        b, dy, dh, half = key
        ref, rs = part(key, i)
        rcopy(ref, ref, s_fwd.at[0], rs, sib).wait_recv()
        if half == 0 and dy == 0:
            to_y(key, i, 1)
            to_y(key, i, -1)
            to_pair(key, i)
        elif half == 0:
            side = {3: 0, 1: 1, 2: b if dh == 0 else 1 - b}[dy]
            d = 1 if side == 0 else -1
            if dy != 2 and (b == side) == (dh == 0):
                to_y(key, i, d)
            to_x(key, i, d)
        if last[key] == n:
            share(key)
        if due and due[0][0] <= n:
            _, bb, group = due.pop(0)
            dots_of(bb, group)
    for _, bb, group in due:
        dots_of(bb, group)

    in_c = acc[0].astype(BF)
    out_t = acc[1].T.reshape(8, 2, 16, TOKP)
    for cc in range(2):
        OT[cc] = out_t[:, cc].reshape(128, TOKP)
    local = ids[...] - T * TURN_G

    def gradient(cc, t):
        lhs = jnp.where(local == t, OT[cc], 0.0).astype(BF)
        return jnp.dot(lhs, in_c, preferred_element_type=F32).reshape(8, 16, RANK)

    for t in range(TURN_G):
        Gs[:, pl.ds(t * 16, 16), :] = gradient(1 - c, t).astype(BF)
    hc = rcopy(Gs, Hin, s_h, r_h, sib)
    hc.start()
    for t in range(TURN_G):
        Gf[:, pl.ds(t * 16, 16), :] = gradient(c, t)
    hc.wait_recv()

    def peer(i, sign):
        far = i < 4
        yy = (y + 4 + sign * jnp.where(far, i, i - 3)) % 4
        return yy * 2 + jnp.where(far, 1 - h, h)

    def rs_copy(i, m, slot):
        return rcopy(Pb.at[m], Rin.at[slot], s_rs.at[i], r_rs.at[slot], (T, m * 2 + c))

    def rs_out(i, _):
        m = peer(i, 1)
        Pb[m] = (Gf[m] + Hin[m].astype(F32)).astype(BF)
        rs_copy(i, m, me).start()
        return 0

    lax.fori_loop(0, 7, rs_out, 0)
    Gf[me] = Gf[me] + Hin[me].astype(F32)
    for cp in sent + shared:
        cp.wait_send()

    @pl.when(edge)
    def _():
        for cp in boundary():
            cp.wait_send()

    hc.wait_send()

    def rs_in(i, _):
        m = peer(6 - i, -1)
        rs_copy(0, m, m).wait_recv()
        Gf[me] = Gf[me] + Rin[m].astype(F32)
        return 0

    lax.fori_loop(0, 7, rs_in, 0)
    for t in range(TURN_G):
        n = cnt_ref[t].astype(F32)
        rows = pl.ds(t * 16, 16)
        Fb[T, rows] = (Gf[me, rows] / n).astype(BF)

    def fz(i, zz, slot):
        return rcopy(Fb.at[slot], Fb.at[slot], s_fz.at[i], r_f.at[slot], (x * 4 + zz, K))

    def fx(i, q, xx, slot):
        return rcopy(
            Fb.at[slot], Fb.at[slot], s_fx.at[q * 4 + i], r_f.at[slot], (xx * 4 + zl, K)
        )

    def unpack(slot):
        rows = pl.ds(pl.multiple_of(slot * 64, 64), 64)
        for half in range(2):
            Ff[half, rows] = Fb[slot, :, half * 128 : (half + 1) * 128].astype(F32)

    for i in range(1, 4):
        fz(i, (zl + i) % 4, T).start()
    for i in range(1, 4):
        fx(i, 0, (x + i) % 4, T).start()
    unpack(T)
    lax.fori_loop(0, 7, lambda i, _: (rs_copy(i, me, me).wait_send(), 0)[1], 0)

    def hand(q, _):
        zz = (zl + 4 - q) % 4
        slot = x * 4 + zz
        fz(q, zz, slot).wait_recv()
        for i in range(1, 4):
            fx(i, q, (x + i) % 4, slot).start()
        unpack(slot)
        return 0

    lax.fori_loop(1, 4, hand, 0)

    def arrive(n, _):
        q, i = n // 3, n % 3 + 1
        slot = ((x + 4 - i) % 4) * 4 + (zl + 4 - q) % 4
        fx(i, q, (x + i) % 4, slot).wait_recv()
        unpack(slot)
        return 0

    lax.fori_loop(0, 12, arrive, 0)
    stored.wait()
    sc = jnp.zeros((128, 64), F32)
    for a in range(16):
        feat = jnp.concatenate(
            [Ff[half, pl.ds(a, 64, stride=16), :] for half in range(2)], axis=1
        ).astype(BF)
        sc = sc + lax.dot_general(
            S[:, a * RANK : (a + 1) * RANK], feat, (((1,), (1,)), ((), ())), preferred_element_type=F32
        )
    rows = sc.reshape(8, 2, 8, 64)
    for cc in range(2):
        Sout[cc, :, :, pl.ds(0, 64)] = rows[:, cc]
    qh = rcopy(Sout.at[1 - c], Qh, s_qh, r_qh, sib)
    qh.start()
    for i in range(1, 4):
        fz(i, (zl + i) % 4, T).wait_send()
        for q in range(4):
            fx(i, q, (x + i) % 4, T).wait_send()
    qh.wait_recv()
    Sc[...] = Sout[c] + Qh[...]

    def q_copy(i, m, slot):
        return rcopy(Sc.at[m], Q.at[slot], s_q.at[i], r_q.at[slot], (T, m * 2 + c))

    def q_out(i, _):
        q_copy(i, peer(i, 1), me).start()
        return 0

    lax.fori_loop(0, 7, q_out, 0)
    qh.wait_send()

    def q_in(i, total):
        m = peer(6 - i, -1)
        q_copy(0, m, m).wait_recv()
        return total + Q[m]

    total = lax.fori_loop(0, 7, q_in, Sc[me])
    out_ref[...] = total[:, :64]
    lax.fori_loop(0, 7, lambda i, _: (q_copy(i, me, me).wait_send(), 0)[1], 0)


def local(
    activations, output_grads, turn_ids, turn_counts, input_basis, output_basis, stored_grads
):
    dma = pltpu.SemaphoreType.DMA
    hbm = pl.BlockSpec(memory_space=pl.ANY)
    out = pl.pallas_call(
        kernel,
        out_shape=jax.ShapeDtypeStruct((8, 64), F32),
        in_specs=[
            pl.BlockSpec(memory_space=pltpu.VMEM),
            pl.BlockSpec(memory_space=pltpu.SMEM),
            hbm,
            hbm,
            hbm,
            hbm,
            hbm,
        ],
        out_specs=pl.BlockSpec(memory_space=pltpu.VMEM),
        scratch_shapes=[
            pltpu.VMEM((2, TOK, D), BF),
            pltpu.VMEM((2, 2, 4, 2, 2, PC, RANK), BF),
            pltpu.VMEM((128, 4096), BF),
            pltpu.VMEM((2, TOKP, RANK), F32),
            pltpu.VMEM((1, TOKP), jnp.int32),
            pltpu.VMEM((2, 128, TOKP), F32),
            pltpu.VMEM((8, 64, RANK), F32),
            pltpu.VMEM((8, 64, RANK), BF),
            pltpu.VMEM((8, 64, RANK), BF),
            pltpu.VMEM((8, 64, RANK), BF),
            pltpu.VMEM((8, 64, RANK), BF),
            pltpu.VMEM((16, 64, RANK), BF),
            pltpu.VMEM((2, 1024, 128), F32),
            pltpu.VMEM((2, 8, 8, 128), F32),
            pltpu.VMEM((8, 8, 128), F32),
            pltpu.VMEM((8, 8, 128), F32),
            pltpu.VMEM((8, 8, 128), F32),
            dma((8,)),
            dma((4,)),
            dma,
            dma((32 * NS,)),
            dma((32,)),
            dma((32,)),
            dma((SEND_MAX,)),
            dma((4 * NS,)),
            dma,
            dma,
            dma((8,)),
            dma((8,)),
            dma((4,)),
            dma((16,)),
            dma((16,)),
            dma,
            dma,
            dma((8,)),
            dma((8,)),
        ],
        compiler_params=pltpu.CompilerParams(
            collective_id=0, has_side_effects=True, vmem_limit_bytes=60 * 1024 * 1024
        ),
        cost_estimate=pl.CostEstimate(
            flops=2 * 1460000000, bytes_accessed=12 * 1024 * 1024, transcendentals=0
        ),
    )(
        turn_ids,
        turn_counts,
        activations,
        output_grads,
        input_basis,
        output_basis,
        stored_grads,
    )
    return out.T


def solution(mesh):
    placed = (
        P(("turn", "tok"), None),
        P(("turn", "tok"), None),
        P(("turn", "tok")),
        P("turn"),
        P("tok", None),
        P("tok", None),
        P("turn", "tok"),
    )
    return jax.shard_map(
        local, mesh=mesh, in_specs=placed, out_specs=P(None, ("turn", "tok")), check_vma=False
    )
```
